512 devices in a mesh: chan: 32 (over z, core), seq: 16 (over x, y).
Axes of the slice: x: 4, y: 4, z: 16, core: 2. Of those that a mesh axis runs over, the one named last changes fastest.
Arguments:
- features: bfloat16 [3, 32768, 4096], P(None, ('seq', 'chan')), may hold values from -6 to 6
- short_taps: float32 [3, 3, 4096], replicated, may hold values from -3 to 3
- decay_rates: float32 [16, 4096], P(None, 'chan'), may hold values from 3.0517579e-06 to 0.03
- residues: float32 [16, 4096], P(None, 'chan'), may hold values from -1.5 to 1.5
- skip_gain: float32 [4096], P('chan'), may hold values from -3 to 3
Outputs:
- gated_out: bfloat16 [32768, 4096], P(('seq', 'chan'))
The draws below stay inside these ranges and needn't reach their ends.
All inputs are finite; a program needn't handle non-finite values.
Results may differ from the reference program's by a relative error of at most 0.0058.
Values may be sent and summed in bfloat16 or wider, within the bound.
A program may use at most 64 MiB of HBM per device.

```python
import math
import jax
import jax.numpy as jnp
from jax import lax

D = 4096
MODES = 16
SHORT = 3
LENGTH = 32768
SUB = 128


def steps_of(stream_key, shape, cuts, low, high):
    gain = 1.0
    for position, blocks in cuts:
        draws = jax.random.uniform(jax.random.fold_in(jax.random.fold_in(stream_key, 6), position), (blocks,), jnp.float32, low / len(cuts), high / len(cuts))
        gain = gain * jnp.repeat(jnp.exp(draws), shape[position] // blocks).reshape((-1,) + (1,) * (len(shape) - 1 - position))
    return gain


def gaussian(rng, dims, scale, bound, cuts=(), kind=jnp.bfloat16):
    drawn = scale * jax.random.normal(rng, dims, jnp.float32)
    if cuts:
        drawn = drawn * steps_of(rng, dims, cuts, -0.22, 0.18)
    return jnp.clip(drawn, -bound, bound).astype(kind)


def setup_inputs(seed: int = 0) -> dict:
    arg_keys = jax.random.split(jax.random.key(seed), 6)
    return {
        "features": gaussian(arg_keys[0], (3, LENGTH, D), 1.0, 6.0, ((1, 512),)),
        "short_taps": gaussian(arg_keys[1], (3, SHORT, D), 0.6, 3.0, (), jnp.float32),
        "decay_rates": jnp.clip(jnp.exp(math.log(0.03) - 9.1932349 * jax.random.uniform(arg_keys[2], (MODES, D), jnp.float32) ** steps_of(arg_keys[2], (MODES, D), ((1, 32),), -0.2, 0.2)), 3.051757857974735e-06, 0.03),
        "residues": gaussian(arg_keys[3], (MODES, D), MODES ** -0.5, 1.5, ((1, 32),), jnp.float32),
        "skip_gain": gaussian(arg_keys[4], (D,), 0.5, 3.0, ((0, 32),), jnp.float32),
    }


def filter_tables(decay_rates, residues, sub_len):
    offsets = jnp.arange(sub_len).astype(decay_rates.dtype)
    powers = jnp.exp(-decay_rates[:, None, :] * offsets[None, :, None])
    weighted = residues * jnp.sqrt(-jnp.expm1(-2.0 * decay_rates))
    impulse = lax.optimization_barrier(jnp.sum(weighted[:, None, :] * powers, axis=0))
    lag_index = (jnp.arange(sub_len)[:, None] - jnp.arange(sub_len)[None, :]).astype(jnp.int32)
    picked = jnp.take(impulse, jnp.maximum(lag_index, 0), axis=0)
    toeplitz = jnp.where((lag_index >= 0)[:, :, None], picked, jnp.zeros_like(picked))
    entry_weight = powers[:, ::-1, :]
    reach_weight = weighted[:, None, :] * powers * jnp.exp(-decay_rates)[:, None, :]
    return (toeplitz, entry_weight, reach_weight)

def short_mix(padded, short_taps):
    count = short_taps.shape[1]
    row_count = padded.shape[1] - (count - 1)
    widened = padded.astype(jnp.float32)
    filtered = jnp.zeros((3, row_count, padded.shape[2]), jnp.float32)
    for shift_by in range(count):
        start_row = count - 1 - shift_by
        filtered = filtered + short_taps[:, shift_by][:, None, :] * widened[:, start_row:start_row + row_count, :]
    gating = filtered[0].astype(jnp.bfloat16)
    product = (filtered[1] * filtered[2]).astype(jnp.bfloat16)
    return (gating, product)

def run_channels(channel_rows, group_taps, group_rates, group_residues, skip_part):
    sub_len = SUB
    padded = jnp.pad(channel_rows, ((0, 0), (SHORT - 1, 0), (0, 0)))
    gating, product = short_mix(padded, group_taps)
    group_width = channel_rows.shape[2]
    z_values = product.astype(jnp.float32).reshape(LENGTH // sub_len, sub_len, group_width)
    toeplitz, entry_weight, reach_weight = filter_tables(group_rates, group_residues, sub_len)
    step_decay = jnp.exp(-group_rates * sub_len)
    highest = lax.Precision.HIGHEST

    def advance(state_in, sub_block):
        outputs = jnp.einsum('tsc,sc->tc', toeplitz, sub_block, precision=highest)
        outputs = outputs + jnp.einsum('mtc,mc->tc', reach_weight, state_in, precision=highest)
        state_out = step_decay * state_in + jnp.einsum('msc,sc->mc', entry_weight, sub_block, precision=highest)
        return (state_out, outputs)
    initial = jnp.zeros((MODES, group_width), jnp.float32)
    _, convolved = lax.scan(advance, initial, z_values)
    convolved = convolved.reshape(LENGTH, group_width)
    result = gating.astype(jnp.float32) * (convolved + skip_part[None, :] * product.astype(jnp.float32))
    return result.astype(jnp.bfloat16)

def reference(features, short_taps, decay_rates, residues, skip_gain):
    groups = 16
    group_width = D // groups
    stacked_rows = features.reshape(3, LENGTH, groups, group_width).transpose(2, 0, 1, 3)
    stacked_taps = short_taps.reshape(3, SHORT, groups, group_width).transpose(2, 0, 1, 3)
    stacked_rates = decay_rates.reshape(MODES, groups, group_width).transpose(1, 0, 2)
    stacked_residues = residues.reshape(MODES, groups, group_width).transpose(1, 0, 2)
    stacked_skip = skip_gain.reshape(groups, group_width)

    def one_group(packed):
        return run_channels(packed[0], packed[1], packed[2], packed[3], packed[4])
    results = lax.map(one_group, (stacked_rows, stacked_taps, stacked_rates, stacked_residues, stacked_skip))
    return results.transpose(1, 0, 2).reshape(LENGTH, D)
```

```python
import functools

import jax
import jax.numpy as jnp
from jax import lax
from jax.experimental import pallas as pl
from jax.experimental.pallas import tpu as pltpu
from jax.sharding import PartitionSpec as P

MESH = pl.DeviceIdType.MESH
LANES = 128
RUNS = 8


def one_minus_exp_neg(u):
    series = 1.0 - u * (1.0 / 8.0)
    for n in (7, 6, 5, 4, 3, 2):
        series = 1.0 - (u * (1.0 / n)) * series
    return jnp.where(u < 0.25, u * series, 1.0 - jnp.exp(-u))


def kernel(
    nz,
    ns,
    taps_ref,
    decay_ref,
    res_ref,
    skip_ref,
    feat_ref,
    out_ref,
    feats,
    tail,
    halo_send,
    halo_recv,
    par_src,
    par_col,
    par_all,
    skip_all,
    wide,
    z_keep,
    g_keep,
    y_keep,
    x_keep,
    e_stage,
    e_recv,
    t_stage,
    t_recv,
    s_stage,
    s_recv,
    o_wide,
    o_keep,
    local_sem,
    pair_send,
    pair_recv,
    tail_sem,
    halo_ssem,
    halo_rsem,
    a_ssem,
    a_rsem,
    k_ssem,
    k_rsem,
    b_ssem,
    b_rsem,
    e_ssem,
    e_rsem,
    t_ssem,
    t_rsem,
    s_ssem,
    s_rsem,
    o_lsem,
    o_ssem,
    o_rsem,
):
    modes = decay_ref.shape[0]
    mp = modes // ns
    rows = feat_ref.shape[1]
    block = 2 * rows
    steps = block // RUNS
    chan = lax.axis_index("chan")
    seq = lax.axis_index("seq")
    z = chan // 2
    k = chan % 2
    other = 1 - k
    position = seq * nz + z
    first = position == 0
    last = position == nz * ns - 1
    f32 = jnp.float32

    def dev(zz, kk, ss):
        return {"chan": zz * 2 + kk, "seq": ss}

    def remote(src, dst, ssem, rsem, device):
        return pltpu.make_async_remote_copy(
            src_ref=src, dst_ref=dst, send_sem=ssem, recv_sem=rsem, device_id=device, device_id_type=MESH
        )

    def local(src, dst, sem):
        return pltpu.make_async_copy(src, dst, sem)

    def wait_bytes(ref, sem):
        pltpu.make_async_copy(ref, ref, sem).wait()

    def far_first(n):
        return (nz // 2 + ((n + 1) // 2) * (1 - 2 * (n % 2))) % nz

    def cols(j, kk):
        return pl.ds(pl.multiple_of((2 * j + kk) * LANES, LANES), LANES)

    my_rows = pl.ds(pl.multiple_of(k * rows, rows), rows)
    other_rows = pl.ds(pl.multiple_of(other * rows, rows), rows)

    barrier = pltpu.get_barrier_semaphore()

    def hello(device):
        pl.semaphore_signal(barrier, inc=1, device_id=device, device_id_type=MESH)

    def hello_z(n, c):
        hello(dev((z + n) % nz, k, seq))
        return c

    def hello_s(n, c):
        hello(dev(z, k, (seq + n) % ns))
        return c

    hello(dev(z, other, seq))
    lax.fori_loop(1, nz, hello_z, 0)
    lax.fori_loop(1, ns, hello_s, 0)
    before = position - 1 + nz * ns
    after = position + 1

    @pl.when(jnp.logical_not(first))
    def _():
        hello(dev(before % nz, 1, (before // nz) % ns))

    sends_halo = jnp.logical_and(k == 1, jnp.logical_not(last))

    def fetch(n, c):
        j = (z + far_first(n)) % nz
        local(feat_ref.at[:, :, cols(j, k)], feats.at[j, :, my_rows, :], local_sem.at[j]).start()
        return c

    @pl.when(sends_halo)
    def _():
        local(feat_ref.at[:, pl.ds(rows - 16, 16), :], tail, tail_sem).start()

    lax.fori_loop(0, nz, fetch, 0)

    decay = decay_ref[...]
    base = jnp.exp(-decay)
    weight = res_ref[...] * jnp.sqrt(one_minus_exp_neg(2.0 * decay))
    for m in range(modes):
        par_src[m, 0:1, :] = base[m : m + 1, :]
        par_src[m, 1:2, :] = weight[m : m + 1, :]

    pl.semaphore_wait(barrier, (nz - 1) + (ns - 1) + 1 + 2 * sends_halo.astype(jnp.int32))

    my_modes = par_src.at[pl.ds(seq * mp, mp)]

    def send_a(n, c):
        remote(my_modes, par_col.at[z], a_ssem, a_rsem, dev((z + far_first(n)) % nz, k, seq)).start()
        return c

    lax.fori_loop(0, nz - 1, send_a, 0)
    local(my_modes, par_col.at[z], a_rsem).start()

    def swap(n, c):
        j = (z + far_first(n)) % nz
        remote(
            feat_ref.at[:, :, cols(j, other)],
            feats.at[j, :, my_rows, :],
            pair_send,
            pair_recv.at[j],
            dev(z, other, seq),
        ).start()
        return c

    lax.fori_loop(0, nz, swap, 0)

    def send_k(n, c):
        remote(skip_ref, skip_all.at[z], k_ssem, k_rsem, dev((z + far_first(n)) % nz, k, seq)).start()
        return c

    lax.fori_loop(0, nz - 1, send_k, 0)
    local(skip_ref, skip_all.at[z], k_rsem).start()

    @pl.when(sends_halo)
    def _():
        local(feat_ref.at[:, pl.ds(rows - 16, 16), :], tail, tail_sem).wait()

        def pick(j, c):
            for kk in range(2):
                for p in range(3):
                    wide_tail = tail[p, :, cols(j, kk)].astype(f32)
                    halo_send[kk, j, 2 * p : 2 * p + 2, :] = wide_tail[14:16, :]
            return c

        lax.fori_loop(0, nz, pick, 0)
        for kk in range(2):
            remote(
                halo_send.at[kk], halo_recv, halo_ssem, halo_rsem, dev(after % nz, kk, (after // nz) % ns)
            ).start()

    wait_bytes(par_col, a_rsem)

    def send_b(n, c):
        remote(par_col, par_all.at[seq], b_ssem, b_rsem, dev(z, k, (seq + n) % ns)).start()
        return c

    lax.fori_loop(1, ns, send_b, 0)
    local(par_col, par_all.at[seq], b_rsem).start()

    @pl.when(first)
    def _():
        halo_recv[...] = jnp.zeros_like(halo_recv)

    @pl.when(jnp.logical_not(first))
    def _():
        wait_bytes(halo_recv, halo_rsem)

    wait_bytes(par_all, b_rsem)
    wait_bytes(skip_all, k_rsem)

    row_id = lax.broadcasted_iota(jnp.int32, (RUNS, LANES), 0)

    def shifted(x, by):
        return jnp.where(row_id >= by, pltpu.roll(x, by, axis=0), 0.0)

    def spread(row):
        return jnp.broadcast_to(row, (RUNS, LANES))

    def par(m, j, which):
        return spread(par_all[m // mp, j, m % mp, which : which + 1, :])

    def run_rows(i):
        return pl.ds(i, RUNS, stride=steps)

    def forward(n, c):
        j = (z + far_first(n)) % nz
        local(feat_ref.at[:, :, cols(j, k)], feats.at[j, :, my_rows, :], local_sem.at[j]).wait()
        remote(
            feat_ref.at[:, :, cols(j, other)],
            feats.at[j, :, other_rows, :],
            pair_send,
            pair_recv.at[j],
            dev(z, other, seq),
        ).wait_recv()
        for p in range(3):
            wide[p] = feats[j, p].astype(f32)
        streams = []
        for p in range(3):
            tap = [spread(taps_ref[p, t : t + 1, cols(j, k)]) for t in range(3)]
            own = [wide[p, run_rows(i), :] for i in range(steps)]
            back1 = jnp.where(row_id == 0, spread(halo_recv[j, 2 * p + 1 : 2 * p + 2, :]), pltpu.roll(own[-1], 1, axis=0))
            back2 = jnp.where(row_id == 0, spread(halo_recv[j, 2 * p : 2 * p + 1, :]), pltpu.roll(own[-2], 1, axis=0))
            seen = [back2, back1] + own
            streams.append(
                [tap[0] * seen[i + 2] + tap[1] * seen[i + 1] + tap[2] * seen[i] for i in range(steps)]
            )
        zs = []
        for i in range(steps):
            g_keep[j, i] = streams[0][i].astype(jnp.bfloat16).astype(f32)
            zs.append((streams[1][i] * streams[2][i]).astype(jnp.bfloat16).astype(f32))
            z_keep[j, i] = zs[i]
        for m in range(modes):
            d = par(m, j, 0)
            acc = zs[0]
            for i in range(1, steps):
                acc = acc * d + zs[i]
            q = d
            reach = 1
            while reach < steps:
                q = q * q
                reach *= 2
            for by in (1, 2, 4):
                acc = acc + q * shifted(acc, by)
                q = q * q
            x_keep[j, m * RUNS : (m + 1) * RUNS, :] = acc
        e_stage[j] = x_keep[j, pl.ds(RUNS - 1, modes, stride=RUNS), :]

        @pl.when(n < nz - 1)
        def _():
            remote(e_stage.at[j], e_recv.at[z], e_ssem, e_rsem, dev(j, k, seq)).start()

        @pl.when(n == nz - 1)
        def _():
            local(e_stage.at[j], e_recv.at[z], e_rsem).start()

        return c

    lax.fori_loop(0, nz, forward, 0)

    def inner(n, c):
        j = (z + far_first(n)) % nz
        taps = [None] * steps
        for m in range(modes):
            d = par(m, j, 0)
            v = par(m, j, 1)
            for i in range(steps):
                taps[i] = v if m == 0 else taps[i] + v
                if i < steps - 1:
                    v = v * d
        taps[0] = taps[0] + spread(skip_all[j])
        zs = [z_keep[j, i] for i in range(steps)]
        for i in range(steps):
            total = taps[0] * zs[i]
            for lag in range(1, i + 1):
                total = total + taps[lag] * zs[i - lag]
            y_keep[j, i] = total
        return c

    lax.fori_loop(0, nz // 2, inner, 0)

    wait_bytes(e_recv, e_rsem)
    block_decay = jnp.exp(-decay * float(block))

    def along_z(zz, state):
        s_stage[zz] = state
        return block_decay * state + e_recv[zz]

    t_stage[...] = lax.fori_loop(0, nz, along_z, jnp.zeros_like(decay))

    def send_t(n, c):
        remote(t_stage, t_recv.at[seq], t_ssem, t_rsem, dev(z, k, (seq + n) % ns)).start()
        return c

    lax.fori_loop(1, ns, send_t, 0)
    local(t_stage, t_recv.at[seq], t_rsem).start()

    lax.fori_loop(nz // 2, nz, inner, 0)

    wait_bytes(t_recv, t_rsem)
    seq_decay = jnp.exp(-decay * float(block * nz))

    def along_s(ss, state):
        return jnp.where(ss < seq, seq_decay * state + t_recv[ss], state)

    incoming = lax.fori_loop(0, ns, along_s, jnp.zeros_like(decay))

    def send_s(n, c):
        zz = (z + far_first(n)) % nz
        s_stage[zz] = s_stage[zz] + jnp.exp(-decay * (zz * block).astype(f32)) * incoming

        @pl.when(n < nz - 1)
        def _():
            remote(s_stage.at[zz], s_recv.at[z], s_ssem, s_rsem.at[z], dev(zz, k, seq)).start()

        @pl.when(n == nz - 1)
        def _():
            local(s_stage.at[zz], s_recv.at[z], s_rsem.at[z]).start()

        return c

    lax.fori_loop(0, nz, send_s, 0)

    def finish(n, c):
        j = (z + far_first(nz - 1 - n)) % nz
        wait_bytes(s_recv.at[j], s_rsem.at[j])
        vs, ds = [], []
        for m in range(modes):
            d = par(m, j, 0)
            q = d
            reach = 1
            while reach < steps:
                q = q * q
                reach *= 2
            q2 = q * q
            power = jnp.where(row_id % 2 == 1, q, 1.0)
            power = power * jnp.where(row_id // 2 % 2 == 1, q2, 1.0)
            power = power * jnp.where(row_id // 4 % 2 == 1, q2 * q2, 1.0)
            start = shifted(x_keep[j, m * RUNS : (m + 1) * RUNS, :], 1) + power * spread(s_recv[j, m : m + 1, :])
            vs.append(par(m, j, 1) * d * start)
            ds.append(d)
        for i in range(steps):
            total = y_keep[j, i]
            for m in range(modes):
                total = total + vs[m]
                if i < steps - 1:
                    vs[m] = vs[m] * ds[m]
            o_wide[run_rows(i), :] = g_keep[j, i] * total
        o_keep[j] = o_wide[...].astype(jnp.bfloat16)
        local(o_keep.at[j, my_rows, :], out_ref.at[:, cols(j, k)], o_lsem).start()
        remote(
            o_keep.at[j, other_rows, :], out_ref.at[:, cols(j, k)], o_ssem, o_rsem, dev(z, other, seq)
        ).start()
        return c

    lax.fori_loop(0, nz, finish, 0)

    half = out_ref.at[:, pl.ds(0, nz * LANES)]
    wait_bytes(half, o_lsem)
    wait_bytes(half, o_ssem)
    wait_bytes(half, o_rsem)
    wait_bytes(feat_ref.at[:, :, pl.ds(0, nz * LANES)], pair_send)
    wait_bytes(par_col.at[pl.ds(0, nz - 1)], a_ssem)
    wait_bytes(skip_all.at[pl.ds(0, nz - 1)], k_ssem)
    wait_bytes(par_all.at[pl.ds(0, ns - 1)], b_ssem)
    wait_bytes(e_recv.at[pl.ds(0, nz - 1)], e_ssem)
    wait_bytes(t_recv.at[pl.ds(0, ns - 1)], t_ssem)
    wait_bytes(s_recv.at[pl.ds(0, nz - 1)], s_ssem)

    @pl.when(sends_halo)
    def _():
        wait_bytes(halo_send, halo_ssem)


def per_device(nz, ns, features, short_taps, decay_rates, residues, skip_gain):
    streams, rows, width = features.shape
    modes = decay_rates.shape[0]
    mp = modes // ns
    block = 2 * rows
    steps = block // RUNS
    f32 = jnp.float32
    vmem = pl.BlockSpec(memory_space=pltpu.VMEM)
    anywhere = pl.BlockSpec(memory_space=pl.ANY)
    dma = pltpu.SemaphoreType.DMA
    return pl.pallas_call(
        functools.partial(kernel, nz, ns),
        out_shape=jax.ShapeDtypeStruct((rows, width), jnp.bfloat16),
        in_specs=[vmem, vmem, vmem, vmem, anywhere],
        out_specs=anywhere,
        scratch_shapes=[
            pltpu.VMEM((nz, streams, block, LANES), jnp.bfloat16),
            pltpu.VMEM((streams, 16, width), jnp.bfloat16),
            pltpu.VMEM((2, nz, 8, LANES), f32),
            pltpu.VMEM((nz, 8, LANES), f32),
            pltpu.VMEM((modes, 2, LANES), f32),
            pltpu.VMEM((nz, mp, 2, LANES), f32),
            pltpu.VMEM((ns, nz, mp, 2, LANES), f32),
            pltpu.VMEM((nz, 1, LANES), f32),
            pltpu.VMEM((streams, block, LANES), f32),
            pltpu.VMEM((nz, steps, RUNS, LANES), f32),
            pltpu.VMEM((nz, steps, RUNS, LANES), f32),
            pltpu.VMEM((nz, steps, RUNS, LANES), f32),
            pltpu.VMEM((nz, modes * RUNS, LANES), f32),
            pltpu.VMEM((nz, modes, LANES), f32),
            pltpu.VMEM((nz, modes, LANES), f32),
            pltpu.VMEM((modes, LANES), f32),
            pltpu.VMEM((ns, modes, LANES), f32),
            pltpu.VMEM((nz, modes, LANES), f32),
            pltpu.VMEM((nz, modes, LANES), f32),
            pltpu.VMEM((block, LANES), f32),
            pltpu.VMEM((nz, block, LANES), jnp.bfloat16),
            dma((nz,)),
            dma,
            dma((nz,)),
            dma,
            dma,
            dma,
            dma,
            dma,
            dma,
            dma,
            dma,
            dma,
            dma,
            dma,
            dma,
            dma,
            dma,
            dma((nz,)),
            dma,
            dma,
            dma,
        ],
        compiler_params=pltpu.CompilerParams(
            collective_id=0, has_side_effects=True, vmem_limit_bytes=24 * 1024 * 1024
        ),
        cost_estimate=pl.CostEstimate(flops=40_000_000, bytes_accessed=2_200_000, transcendentals=0),
    )(short_taps, decay_rates, residues, skip_gain.reshape(1, -1), features)


def solution(mesh):
    nz, ns = mesh.shape["chan"] // 2, mesh.shape["seq"]
    placed = (P(None, ("seq", "chan"), None), P(), P(None, "chan"), P(None, "chan"), P("chan"))
    return jax.shard_map(
        functools.partial(per_device, nz, ns),
        mesh=mesh,
        in_specs=placed,
        out_specs=P(("seq", "chan"), None),
        check_vma=False,
    )
```

```python
import functools

import jax
import jax.numpy as jnp
import ml_dtypes
import numpy as np
from jax import lax
from jax.experimental import pallas as pl
from jax.experimental.pallas import tpu as pltpu
from jax.sharding import PartitionSpec as P

MESH = pl.DeviceIdType.MESH
LANES = 128
RUNS = 8
TERMS = 12
GROUP = 4


def fixed_matrices(block):
    steps = block // RUNS
    rows = np.arange(block)
    token = steps * (rows % RUNS) + rows // RUNS

    def polys(lag):
        u = 2.0 * lag / block - 1.0
        out = [np.ones_like(u), u]
        while len(out) < TERMS:
            out.append(2.0 * u * out[-1] - out[-2])
        return np.stack(out)

    def parts(x):
        found = []
        for _ in range(3):
            found.append(x.astype(ml_dtypes.bfloat16))
            x = x - found[-1].astype(np.float64)
        return found

    lag = token[:, None] - token[None, :]
    inside = np.where(lag >= 0, polys(np.maximum(lag, 0).astype(np.float64)), 0.0)
    first, second, _ = parts(inside.reshape(TERMS * block, block))
    toeplitz = np.stack([first, second])

    end = np.zeros((16, block))
    end[:TERMS] = polys((block - 1 - token).astype(np.float64))
    first, second, third = parts(end)
    moments = np.stack([np.concatenate([first, third]), np.concatenate([second, 0 * third])])

    reach = np.zeros((block, 16))
    reach[:, :TERMS] = polys((token + 1).astype(np.float64)).T
    first, second, _ = parts(reach)
    none = 0 * first
    cross = np.concatenate([first, first, first, second, second, none, none, none], axis=1)
    return toeplitz, moments, cross


def one_minus_exp_neg(u):
    series = 1.0 - u * (1.0 / 8.0)
    for n in (7, 6, 5, 4, 3, 2):
        series = 1.0 - (u * (1.0 / n)) * series
    return jnp.where(u < 0.25, u * series, 1.0 - jnp.exp(-u))


def kernel(
    nz,
    ns,
    taps_hbm,
    decay_hbm,
    res_hbm,
    skip_hbm,
    toep_hbm,
    mom_hbm,
    cross_hbm,
    feat_ref,
    out_ref,
    taps_ref,
    decay_ref,
    res_ref,
    skip_ref,
    toep_ref,
    mom_ref,
    cross_ref,
    feats,
    tail,
    halo_send,
    halo_recv,
    h_src,
    h_col,
    h_all,
    c_keep,
    wide,
    z_keep,
    g_keep,
    u_keep,
    y_keep,
    e_stage,
    e_recv,
    p_keep,
    t_stage,
    t_recv,
    r_stage,
    r_recv,
    r_flat,
    o_wide,
    o_keep,
    arg_sem,
    local_sem,
    pair_send,
    pair_recv,
    tail_sem,
    halo_ssem,
    halo_rsem,
    a_ssem,
    a_rsem,
    b_ssem,
    b_rsem,
    e_ssem,
    e_rsem,
    t_ssem,
    t_rsem,
    r_ssem,
    r_rsem,
    o_lsem,
    o_ssem,
    o_rsem,
):
    modes = decay_hbm.shape[0]
    share = 16 // ns
    rows = feat_ref.shape[1]
    block = 2 * rows
    steps = block // RUNS
    chan = lax.axis_index("chan")
    seq = lax.axis_index("seq")
    z = chan // 2
    k = chan % 2
    other = 1 - k
    position = seq * nz + z
    first = position == 0
    last = position == nz * ns - 1
    f32 = jnp.float32

    def dev(zz, kk, ss):
        return {"chan": zz * 2 + kk, "seq": ss}

    def remote(src, dst, ssem, rsem, device):
        return pltpu.make_async_remote_copy(
            src_ref=src, dst_ref=dst, send_sem=ssem, recv_sem=rsem, device_id=device, device_id_type=MESH
        )

    def local(src, dst, sem):
        return pltpu.make_async_copy(src, dst, sem)

    def wait_bytes(ref, sem):
        pltpu.make_async_copy(ref, ref, sem).wait()

    def far_first(n, of=nz):
        return (of // 2 + ((n + 1) // 2) * (1 - 2 * (n % 2))) % of

    def cols(j, kk):
        return pl.ds(pl.multiple_of((2 * j + kk) * LANES, LANES), LANES)

    my_rows = pl.ds(pl.multiple_of(k * rows, rows), rows)
    other_rows = pl.ds(pl.multiple_of(other * rows, rows), rows)

    barrier = pltpu.get_barrier_semaphore()

    def hello(device):
        pl.semaphore_signal(barrier, inc=1, device_id=device, device_id_type=MESH)

    def hello_z(n, c):
        hello(dev((z + far_first(n)) % nz, k, seq))
        return c

    def hello_s(n, c):
        hello(dev(z, k, (seq + n) % ns))
        return c

    lax.fori_loop(0, nz - 1, hello_z, 0)
    lax.fori_loop(1, ns, hello_s, 0)
    hello(dev(z, other, seq))
    before = position - 1 + nz * ns
    after = position + 1

    @pl.when(jnp.logical_not(first))
    def _():
        hello(dev(before % nz, 1, (before // nz) % ns))

    sends_halo = jnp.logical_and(k == 1, jnp.logical_not(last))

    def fetch(n, c):
        j = (z + far_first(n)) % nz
        local(feat_ref.at[:, :, cols(j, k)], feats.at[j, :, my_rows, :], local_sem.at[j]).start()
        return c

    left, right = slice(0, block), slice(block, 2 * block)
    smalls = [
        (decay_hbm, decay_ref),
        (res_hbm, res_ref),
        (skip_hbm, skip_ref),
        (taps_hbm, taps_ref),
        (mom_hbm.at[0], mom_ref.at[:, left]),
        (mom_hbm.at[1], mom_ref.at[:, right]),
        (toep_hbm.at[0], toep_ref.at[:, left]),
        (toep_hbm.at[1], toep_ref.at[:, right]),
        (cross_hbm, cross_ref),
    ]

    def ready(numbers):
        for i in numbers:
            local(*smalls[i], arg_sem.at[i]).wait()

    for i, (src, dst) in enumerate(smalls[:3]):
        local(src, dst, arg_sem.at[i]).start()

    @pl.when(sends_halo)
    def _():
        local(feat_ref.at[:, pl.ds(rows - 16, 16), :], tail, tail_sem).start()

    lax.fori_loop(0, nz, fetch, 0)
    for i, (src, dst) in enumerate(smalls[3:]):
        local(src, dst, arg_sem.at[3 + i]).start()

    ready((0, 1, 2))
    decay = decay_ref[...]
    weight = res_ref[...] * jnp.sqrt(one_minus_exp_neg(2.0 * decay))
    half_a = decay * (block / 4.0)
    square = half_a * half_a
    lead = jnp.exp(-2.0 * half_a)
    for t in range(TERMS):
        total = jnp.ones_like(square)
        for i in range(10, 0, -1):
            total = 1.0 + square * (1.0 / (i * (i + t))) * total
        coef = lead * total * (1.0 if t == 0 else 2.0)
        lead = lead * half_a * (-1.0 / (t + 1))
        c_keep[0, t] = coef
        c_keep[1, t] = weight * coef
        h_src[t] = jnp.sum(weight * coef, axis=0, keepdims=True)
    for t in range(TERMS, 16):
        h_src[t] = skip_ref[...]
    r_flat[...] = jnp.zeros_like(r_flat)

    @pl.when(sends_halo)
    def _():
        local(feat_ref.at[:, pl.ds(rows - 16, 16), :], tail, tail_sem).wait()

        def pick(j, c):
            for kk in range(2):
                for q in range(3):
                    wide_tail = tail[q, :, cols(j, kk)].astype(f32)
                    halo_send[kk, j, q] = wide_tail[14:16, :]
            return c

        lax.fori_loop(0, nz, pick, 0)

    pl.semaphore_wait(barrier, (nz - 1) + (ns - 1) + 1 + 2 * sends_halo.astype(jnp.int32))

    @pl.when(sends_halo)
    def _():
        for kk in range(2):
            remote(
                halo_send.at[kk], halo_recv, halo_ssem, halo_rsem, dev(after % nz, kk, (after // nz) % ns)
            ).start()

    def swap(n, c):
        j = (z + far_first(n)) % nz
        remote(
            feat_ref.at[:, :, cols(j, other)],
            feats.at[j, :, my_rows, :],
            pair_send,
            pair_recv.at[j],
            dev(z, other, seq),
        ).start()
        return c

    lax.fori_loop(0, nz, swap, 0)

    my_rows_h = h_src.at[pl.ds(seq * share, share)]

    def send_a(n, c):
        remote(my_rows_h, h_col.at[z], a_ssem, a_rsem, dev((z + far_first(n)) % nz, k, seq)).start()
        return c

    lax.fori_loop(0, nz - 1, send_a, 0)
    local(my_rows_h, h_col.at[z], a_rsem).start()

    @pl.when(first)
    def _():
        halo_recv[...] = jnp.zeros_like(halo_recv)

    @pl.when(jnp.logical_not(first))
    def _():
        wait_bytes(halo_recv, halo_rsem)

    ready((3, 4, 5))

    row_id = lax.broadcasted_iota(jnp.int32, (RUNS, LANES), 0)

    def spread(row):
        return jnp.broadcast_to(row, (RUNS, LANES))

    def run_rows(i):
        return pl.ds(i, RUNS, stride=steps)

    def term(ref, j, t):
        return ref[j, t // GROUP, t % GROUP : t % GROUP + 1, :]

    def conv(j, p, lanes):
        local(feat_ref.at[:, :, cols(j, k)], feats.at[j, :, my_rows, :], local_sem.at[j]).wait()
        remote(
            feat_ref.at[:, :, cols(j, other)],
            feats.at[j, :, other_rows, :],
            pair_send,
            pair_recv.at[j],
            dev(z, other, seq),
        ).wait_recv()
        for q in range(3):
            wide[q] = feats[j, q].astype(f32)
        streams = []
        for q in range(3):
            tap = [spread(taps_ref[q, t : t + 1, cols(j, k)]) for t in range(3)]
            own = [wide[q, run_rows(i), :] for i in range(steps)]
            back1 = jnp.where(row_id == 0, spread(halo_recv[j, q, 1:2, :]), pltpu.roll(own[-1], 1, axis=0))
            back2 = jnp.where(row_id == 0, spread(halo_recv[j, q, 0:1, :]), pltpu.roll(own[-2], 1, axis=0))
            seen = [back2, back1] + own
            streams.append(
                [tap[0] * seen[i + 2] + tap[1] * seen[i + 1] + tap[2] * seen[i] for i in range(steps)]
            )
        for i in range(steps):
            g_keep[j, i * RUNS : (i + 1) * RUNS, :] = streams[0][i].astype(jnp.bfloat16).astype(f32)
        product = jnp.concatenate([streams[1][i] * streams[2][i] for i in range(steps)], axis=0).astype(jnp.bfloat16)
        z_keep[p, 0:block, lanes] = product
        z_keep[p, block : 2 * block, lanes] = product

    def forward(n, c):
        p = (z // 2 + far_first(n, nz // 2)) % (nz // 2)
        for h in range(2):
            conv(2 * p + h, p, pl.ds(h * LANES, LANES))
        found = jnp.dot(mom_ref[...], z_keep[p], preferred_element_type=f32)
        found = found[0:16] + found[16:32]
        for h in range(2):
            j = 2 * p + h
            for a in range(TERMS // GROUP):
                e_stage[j, a] = found[a * GROUP : (a + 1) * GROUP, h * LANES : (h + 1) * LANES]

            @pl.when(j != z)
            def _():
                remote(e_stage.at[j], e_recv.at[z], e_ssem, e_rsem, dev(j, k, seq)).start()

            @pl.when(j == z)
            def _():
                local(e_stage.at[j], e_recv.at[z], e_rsem).start()

        return c

    lax.fori_loop(0, nz // 2, forward, 0)

    def inner(p, c):
        u_keep[...] = jnp.dot(toep_ref[...], z_keep[p], preferred_element_type=f32)
        for h in range(2):
            j = 2 * p + h
            lanes = slice(h * LANES, (h + 1) * LANES)
            hs = [spread(h_all[t // share, j, t % share]) for t in range(TERMS)]
            skip = spread(h_all[TERMS // share, j, TERMS % share])
            for i in range(0, steps, 2):
                kept = z_keep[p, i * RUNS : (i + 2) * RUNS, lanes].astype(f32)
                for b in range(2):
                    row = (i + b) * RUNS
                    total = skip * kept[b * RUNS : (b + 1) * RUNS]
                    for t in range(TERMS):
                        total = total + hs[t] * u_keep[t * block + row : t * block + row + RUNS, lanes]
                    y_keep[j, row : row + RUNS, :] = total
        return c

    wait_bytes(h_col, a_rsem)

    def send_b(n, c):
        remote(h_col, h_all.at[seq], b_ssem, b_rsem, dev(z, k, (seq + n) % ns)).start()
        return c

    lax.fori_loop(1, ns, send_b, 0)
    local(h_col, h_all.at[seq], b_rsem).start()

    wait_bytes(e_recv, e_rsem)
    block_decay = jnp.exp(-decay * float(block))

    def along_z(zz, state):
        p_keep[zz] = state
        added = c_keep[0, 0] * term(e_recv, zz, 0)
        for t in range(1, TERMS):
            added = added + c_keep[0, t] * term(e_recv, zz, t)
        return block_decay * state + added

    t_stage[...] = lax.fori_loop(0, nz, along_z, jnp.zeros_like(decay))

    def send_t(ss, c):
        remote(t_stage, t_recv.at[seq], t_ssem.at[ss], t_rsem.at[seq], dev(z, k, ss)).start()
        return c

    lax.fori_loop(seq + 1, ns, send_t, 0)

    wait_bytes(h_all, b_rsem)
    ready((6, 7, 8))
    lax.fori_loop(0, nz // 4, inner, 0)

    seq_decay = jnp.exp(-decay * float(block * nz))

    def along_s(ss, state):
        wait_bytes(t_recv.at[ss], t_rsem.at[ss])
        return seq_decay * state + t_recv[ss]

    incoming = lax.fori_loop(0, seq, along_s, jnp.zeros_like(decay))

    def send_r(n, c):
        zz = (z + far_first(n)) % nz
        state = p_keep[zz] + jnp.exp(-decay * (zz * block).astype(f32)) * incoming
        for t in range(TERMS):
            r_stage[zz, t // GROUP, t % GROUP : t % GROUP + 1, :] = jnp.sum(c_keep[1, t] * state, axis=0, keepdims=True)

        @pl.when(n < nz - 1)
        def _():
            remote(r_stage.at[zz], r_recv.at[z], r_ssem, r_rsem.at[z], dev(zz, k, seq)).start()

        @pl.when(n == nz - 1)
        def _():
            local(r_stage.at[zz], r_recv.at[z], r_rsem.at[z]).start()

        return c

    lax.fori_loop(0, nz, send_r, 0)
    lax.fori_loop(nz // 4, nz // 2, inner, 0)

    def finish(n, c):
        p = (z // 2 + far_first(nz // 2 - 1 - n, nz // 2)) % (nz // 2)
        for h in range(2):
            j = 2 * p + h
            wait_bytes(r_recv.at[j], r_rsem.at[j])
            for a in range(TERMS // GROUP):
                r_flat[a * GROUP : (a + 1) * GROUP, h * LANES : (h + 1) * LANES] = r_recv[j, a]
        coef = r_flat[...]
        one = coef.astype(jnp.bfloat16)
        rest = coef - one.astype(f32)
        two = rest.astype(jnp.bfloat16)
        three = (rest - two.astype(f32)).astype(jnp.bfloat16)
        none = jnp.zeros_like(one)
        stacked = jnp.concatenate([one, two, three, one, two, none, none, none], axis=0)
        reached = jnp.dot(cross_ref[...], stacked, preferred_element_type=f32)
        for h in range(2):
            j = 2 * p + h
            for i in range(steps):
                at = slice(i * RUNS, (i + 1) * RUNS)
                o_wide[h, run_rows(i), :] = g_keep[j, at, :] * (
                    y_keep[j, at, :] + reached[at, h * LANES : (h + 1) * LANES]
                )
            o_keep[j] = o_wide[h].astype(jnp.bfloat16)
            local(o_keep.at[j, my_rows, :], out_ref.at[:, cols(j, k)], o_lsem).start()
            remote(
                o_keep.at[j, other_rows, :], out_ref.at[:, cols(j, k)], o_ssem, o_rsem, dev(z, other, seq)
            ).start()
        return c

    lax.fori_loop(0, nz // 2, finish, 0)

    half = out_ref.at[:, pl.ds(0, nz * LANES)]
    wait_bytes(half, o_lsem)
    wait_bytes(half, o_ssem)
    wait_bytes(half, o_rsem)
    wait_bytes(feat_ref.at[:, :, pl.ds(0, nz * LANES)], pair_send)
    wait_bytes(h_col.at[pl.ds(0, nz - 1)], a_ssem)
    wait_bytes(h_all.at[pl.ds(0, ns - 1)], b_ssem)
    wait_bytes(e_recv.at[pl.ds(0, nz - 1)], e_ssem)

    def sent_t(ss, c):
        wait_bytes(t_stage, t_ssem.at[ss])
        return c

    lax.fori_loop(seq + 1, ns, sent_t, 0)
    wait_bytes(r_recv.at[pl.ds(0, nz - 1)], r_ssem)

    @pl.when(sends_halo)
    def _():
        wait_bytes(halo_send, halo_ssem)


def per_device(nz, ns, features, short_taps, decay_rates, residues, skip_gain):
    streams, rows, width = features.shape
    modes = decay_rates.shape[0]
    block = 2 * rows
    groups = TERMS // GROUP
    toeplitz, moments, cross = fixed_matrices(block)
    f32 = jnp.float32
    bf16 = jnp.bfloat16
    hbm = pl.BlockSpec(memory_space=pltpu.HBM)
    anywhere = pl.BlockSpec(memory_space=pl.ANY)
    dma = pltpu.SemaphoreType.DMA
    return pl.pallas_call(
        functools.partial(kernel, nz, ns),
        out_shape=jax.ShapeDtypeStruct((rows, width), jnp.bfloat16),
        in_specs=[hbm] * 8,
        out_specs=anywhere,
        scratch_shapes=[
            pltpu.VMEM(short_taps.shape, f32),
            pltpu.VMEM((modes, LANES), f32),
            pltpu.VMEM((modes, LANES), f32),
            pltpu.VMEM((1, LANES), f32),
            pltpu.VMEM((TERMS * block, 2 * block), bf16),
            pltpu.VMEM((32, 2 * block), bf16),
            pltpu.VMEM(cross.shape, bf16),
            pltpu.VMEM((nz, streams, block, LANES), bf16),
            pltpu.VMEM((streams, 16, width), bf16),
            pltpu.VMEM((2, nz, streams, 2, LANES), f32),
            pltpu.VMEM((nz, streams, 2, LANES), f32),
            pltpu.VMEM((16, 1, LANES), f32),
            pltpu.VMEM((nz, 16 // ns, 1, LANES), f32),
            pltpu.VMEM((ns, nz, 16 // ns, 1, LANES), f32),
            pltpu.VMEM((2, TERMS, modes, LANES), f32),
            pltpu.VMEM((streams, block, LANES), f32),
            pltpu.VMEM((nz // 2, 2 * block, 2 * LANES), bf16),
            pltpu.VMEM((nz, block, LANES), f32),
            pltpu.VMEM((TERMS * block, 2 * LANES), f32),
            pltpu.VMEM((nz, block, LANES), f32),
            pltpu.VMEM((nz, groups, GROUP, LANES), f32),
            pltpu.VMEM((nz, groups, GROUP, LANES), f32),
            pltpu.VMEM((nz, modes, LANES), f32),
            pltpu.VMEM((modes, LANES), f32),
            pltpu.VMEM((ns, modes, LANES), f32),
            pltpu.VMEM((nz, groups, GROUP, LANES), f32),
            pltpu.VMEM((nz, groups, GROUP, LANES), f32),
            pltpu.VMEM((16, 2 * LANES), f32),
            pltpu.VMEM((2, block, LANES), f32),
            pltpu.VMEM((nz, block, LANES), bf16),
            dma((9,)),
            dma((nz,)),
            dma,
            dma((nz,)),
            dma,
            dma,
            dma,
            dma,
            dma,
            dma,
            dma,
            dma,
            dma,
            dma((ns,)),
            dma((ns,)),
            dma,
            dma((nz,)),
            dma,
            dma,
            dma,
        ],
        compiler_params=pltpu.CompilerParams(
            collective_id=0, has_side_effects=True, vmem_limit_bytes=60 * 1024 * 1024
        ),
        cost_estimate=pl.CostEstimate(flops=40_000_000, bytes_accessed=2_200_000, transcendentals=0),
    )(short_taps, decay_rates, residues, skip_gain.reshape(1, -1), toeplitz, moments, cross, features)


def solution(mesh):
    nz, ns = mesh.shape["chan"] // 2, mesh.shape["seq"]
    placed = (P(None, ("seq", "chan"), None), P(), P(None, "chan"), P(None, "chan"), P("chan"))
    return jax.shard_map(
        functools.partial(per_device, nz, ns),
        mesh=mesh,
        in_specs=placed,
        out_specs=P(("seq", "chan"), None),
        check_vma=False,
    )
```

```python
import functools

import jax
import jax.numpy as jnp
import ml_dtypes
import numpy as np
from jax import lax
from jax.experimental import pallas as pl
from jax.experimental.pallas import tpu as pltpu
from jax.sharding import PartitionSpec as P

MESH = pl.DeviceIdType.MESH
LANES = 128
RUNS = 8
TERMS = 12


def fixed_matrices(block):
    half = block // 2
    steps = half // RUNS
    rows = np.arange(half)
    token = steps * (rows % RUNS) + rows // RUNS
    token = np.concatenate([token, half + token])

    def polys(lag):
        u = 2.0 * lag / block - 1.0
        out = [np.ones_like(u), u]
        while len(out) < TERMS:
            out.append(2.0 * u * out[-1] - out[-2])
        return np.stack(out)

    def parts(x):
        found = []
        for _ in range(3):
            found.append(x.astype(ml_dtypes.bfloat16))
            x = x - found[-1].astype(np.float64)
        return found

    lag = token[:, None] - token[None, :]
    inside = np.where(lag >= 0, polys(np.maximum(lag, 0).astype(np.float64)), 0.0)
    first, second, _ = parts(inside.reshape(TERMS * block, block))
    toeplitz = np.stack([first, second])

    end = np.zeros((16, block))
    end[:TERMS] = polys((block - 1 - token).astype(np.float64))
    first, second, third = parts(end)
    moments = np.stack([np.concatenate([first, third]), np.concatenate([second, 0 * third])])

    reach = np.zeros((block, 16))
    reach[:, :TERMS] = polys((token + 1).astype(np.float64)).T
    first, second, _ = parts(reach)
    none = 0 * first
    cross = np.concatenate([first, second] + [none] * 6, axis=1)
    return toeplitz, moments, cross


def one_minus_exp_neg(u):
    series = 1.0 - u * (1.0 / 8.0)
    for n in (7, 6, 5, 4, 3, 2):
        series = 1.0 - (u * (1.0 / n)) * series
    return jnp.where(u < 0.25, u * series, 1.0 - jnp.exp(-u))


def kernel(
    nz,
    ns,
    taps_hbm,
    decay_hbm,
    res_hbm,
    skip_hbm,
    toep_hbm,
    mom_hbm,
    cross_hbm,
    feat_ref,
    out_ref,
    taps_ref,
    decay_ref,
    res_ref,
    skip_ref,
    toep_ref,
    mom_ref,
    cross_ref,
    feats,
    halo_send,
    halo_recv,
    edge_out,
    edges,
    z_out,
    g_out,
    h_src,
    h_col,
    h_all,
    c_keep,
    wide,
    z_keep,
    g_keep,
    u_keep,
    y_keep,
    e_stage,
    e_recv,
    p_keep,
    t_stage,
    t_recv,
    r_stage,
    r_recv,
    r_flat,
    o_wide,
    o_keep,
    arg_sem,
    local_sem,
    z_ssem,
    z_rsem,
    g_ssem,
    g_rsem,
    edge_ssem,
    edge_rsem,
    halo_ssem,
    halo_rsem,
    a_ssem,
    a_rsem,
    b_ssem,
    b_rsem,
    e_ssem,
    e_rsem,
    t_ssem,
    t_rsem,
    r_ssem,
    r_rsem,
    o_lsem,
    o_ssem,
    o_rsem,
):
    modes = decay_hbm.shape[0]
    share = 16 // ns
    rows = feat_ref.shape[1]
    block = 2 * rows
    steps = rows // RUNS
    pairs = nz // 2
    chan = lax.axis_index("chan")
    seq = lax.axis_index("seq")
    z = chan // 2
    k = chan % 2
    other = 1 - k
    position = seq * nz + z
    first = position == 0
    last = position == nz * ns - 1
    f32 = jnp.float32

    def dev(zz, kk, ss):
        return {"chan": zz * 2 + kk, "seq": ss}

    def remote(src, dst, ssem, rsem, device):
        return pltpu.make_async_remote_copy(
            src_ref=src, dst_ref=dst, send_sem=ssem, recv_sem=rsem, device_id=device, device_id_type=MESH
        )

    def local(src, dst, sem):
        return pltpu.make_async_copy(src, dst, sem)

    def wait_bytes(ref, sem):
        pltpu.make_async_copy(ref, ref, sem).wait()

    def far_first(n, of=nz):
        return (of // 2 + ((n + 1) // 2) * (1 - 2 * (n % 2))) % of

    def cols(j, kk):
        return pl.ds(pl.multiple_of((2 * j + kk) * LANES, LANES), LANES)

    my_rows = pl.ds(pl.multiple_of(k * rows, rows), rows)
    other_rows = pl.ds(pl.multiple_of(other * rows, rows), rows)

    barrier = pltpu.get_barrier_semaphore()

    def hello(device):
        pl.semaphore_signal(barrier, inc=1, device_id=device, device_id_type=MESH)

    def hello_z(n, c):
        hello(dev((z + far_first(n)) % nz, k, seq))
        return c

    def hello_s(n, c):
        hello(dev(z, k, (seq + n) % ns))
        return c

    lax.fori_loop(0, nz - 1, hello_z, 0)
    lax.fori_loop(1, ns, hello_s, 0)
    hello(dev(z, other, seq))
    before = position - 1 + nz * ns
    after = position + 1

    @pl.when(jnp.logical_not(first))
    def _():
        hello(dev(before % nz, 1, (before // nz) % ns))

    sends_halo = jnp.logical_and(k == 1, jnp.logical_not(last))

    wide_cols = 4 * LANES

    def chunk(p):
        at = pl.ds(pl.multiple_of(p * wide_cols, wide_cols), wide_cols)
        return local(feat_ref.at[:, :, at], feats.at[p], local_sem.at[p])

    def fetch(p, c):
        chunk(p).start()
        return c

    left, right = slice(0, block), slice(block, 2 * block)
    smalls = [
        (taps_hbm, taps_ref),
        (decay_hbm, decay_ref),
        (res_hbm, res_ref),
        (skip_hbm, skip_ref),
        (mom_hbm.at[0], mom_ref.at[:, left]),
        (mom_hbm.at[1], mom_ref.at[:, right]),
        (toep_hbm.at[0], toep_ref.at[:, left]),
        (toep_hbm.at[1], toep_ref.at[:, right]),
        (cross_hbm, cross_ref),
    ]

    def ready(numbers):
        for i in numbers:
            local(*smalls[i], arg_sem.at[i]).wait()

    local(*smalls[0], arg_sem.at[0]).start()
    lax.fori_loop(0, pairs, fetch, 0)
    for i, (src, dst) in enumerate(smalls[1:]):
        local(src, dst, arg_sem.at[1 + i]).start()
    ready((0,))

    row_id = lax.broadcasted_iota(jnp.int32, (RUNS, LANES), 0)

    def spread(row):
        return jnp.broadcast_to(row, (RUNS, LANES))

    def run_rows(i, base=0):
        return pl.ds(base + i, RUNS, stride=steps)

    def conv(p, c):
        chunk(p).wait()
        for h in range(2):
            j = 2 * p + h
            for mine in (True, False):
                kk = k if mine else other
                at = pl.ds(pl.multiple_of((2 * h + kk) * LANES, LANES), LANES)
                streams = []
                for q in range(3):
                    wide[q] = feats[p, q, :, at].astype(f32)
                    tap = [spread(taps_ref[q, t : t + 1, cols(j, kk)]) for t in range(3)]
                    own = [wide[q, run_rows(i), :] for i in range(steps)]
                    seen = [pltpu.roll(own[-2], 1, axis=0), pltpu.roll(own[-1], 1, axis=0)] + own
                    streams.append(
                        [tap[0] * seen[i + 2] + tap[1] * seen[i + 1] + tap[2] * seen[i] for i in range(steps)]
                    )
                    ends = [wide[q, 0:2, :], wide[q, rows - 2 : rows, :]]
                    kept = edges.at[k] if mine else edge_out
                    kept[j, q, 0:2, :] = ends[0]
                    kept[j, q, 2:4, :] = ends[1]
                    halo_send[kk, j, q] = ends[1]
                gate = jnp.concatenate(streams[0], axis=0).astype(jnp.bfloat16)
                product = jnp.concatenate([streams[1][i] * streams[2][i] for i in range(steps)], axis=0)
                product = product.astype(jnp.bfloat16)
                lanes = pl.ds(h * LANES, LANES)
                if mine:
                    z_keep[p, my_rows, lanes] = product
                    g_keep[j, my_rows, :] = gate
                else:
                    z_out[p, :, lanes] = product
                    g_out[j] = gate
        return c

    lax.fori_loop(0, pairs, conv, 0)

    ready((1, 2, 3))
    decay = decay_ref[...]
    weight = res_ref[...] * jnp.sqrt(one_minus_exp_neg(2.0 * decay))
    half_a = decay * (block / 4.0)
    square = half_a * half_a
    lead = jnp.exp(-2.0 * half_a)
    for t in range(TERMS):
        total = jnp.ones_like(square)
        for i in range(10, 0, -1):
            total = 1.0 + square * (1.0 / (i * (i + t))) * total
        coef = lead * total * (1.0 if t == 0 else 2.0)
        lead = lead * half_a * (-1.0 / (t + 1))
        c_keep[0, t] = coef
        c_keep[1, t] = weight * coef
        h_src[t] = jnp.sum(weight * coef, axis=0, keepdims=True)
    for t in range(TERMS, 16):
        h_src[t] = skip_ref[...]
    r_flat[...] = jnp.zeros_like(r_flat)

    pl.semaphore_wait(barrier, (nz - 1) + (ns - 1) + 1 + 2 * sends_halo.astype(jnp.int32))

    @pl.when(sends_halo)
    def _():
        for kk in range(2):
            remote(
                halo_send.at[kk], halo_recv, halo_ssem, halo_rsem, dev(after % nz, kk, (after // nz) % ns)
            ).start()

    edge_copy = remote(edge_out, edges.at[k], edge_ssem, edge_rsem, dev(z, other, seq))
    edge_copy.start()

    def z_copy(p):
        return remote(z_out.at[p], z_keep.at[p, my_rows, :], z_ssem, z_rsem.at[p], dev(z, other, seq))

    def swap(n, c):
        z_copy((z // 2 + far_first(n, pairs)) % pairs).start()
        return c

    lax.fori_loop(0, pairs, swap, 0)

    my_rows_h = h_src.at[pl.ds(seq * share, share)]

    def send_a(n, c):
        remote(my_rows_h, h_col.at[z], a_ssem, a_rsem, dev((z + far_first(n)) % nz, k, seq)).start()
        return c

    lax.fori_loop(0, nz - 1, send_a, 0)
    local(my_rows_h, h_col.at[z], a_rsem).start()

    remote(g_out, g_keep.at[:, my_rows, :], g_ssem, g_rsem, dev(z, other, seq)).start()

    @pl.when(first)
    def _():
        halo_recv[...] = jnp.zeros_like(halo_recv)

    @pl.when(jnp.logical_not(first))
    def _():
        wait_bytes(halo_recv, halo_rsem)

    ready((4, 5))
    wait_bytes(edge_out, edge_rsem)

    def two_first(q, j, h):
        now = edges[h, j, q, 0:2, :]
        past = halo_recv[j, q] if h == 0 else edges[0, j, q, 2:4, :]
        tap = [taps_ref[q, t : t + 1, cols(j, k)] for t in range(3)]
        one = tap[0] * now[0:1] + tap[1] * past[1:2] + tap[2] * past[0:1]
        two = tap[0] * now[1:2] + tap[1] * now[0:1] + tap[2] * past[1:2]
        return one, two

    tile_row = lax.broadcasted_iota(jnp.int32, (16, LANES), 0)

    def mend(old, one, two):
        fresh = jnp.where(tile_row == 0, jnp.broadcast_to(one, (16, LANES)), old.astype(f32))
        fresh = jnp.where(tile_row == RUNS, jnp.broadcast_to(two, (16, LANES)), fresh)
        return fresh.astype(jnp.bfloat16)

    def forward(n, c):
        p = (z // 2 + far_first(n, pairs)) % pairs
        wait_bytes(z_out.at[p], z_rsem.at[p])
        for h in range(2):
            lanes = pl.ds(h * LANES, LANES)
            for core in range(2):
                at = pl.ds(core * rows, 16)
                second, third = two_first(1, 2 * p + h, core), two_first(2, 2 * p + h, core)
                z_keep[p, at, lanes] = mend(z_keep[p, at, lanes], second[0] * third[0], second[1] * third[1])
        kept = z_keep[p]
        found = jnp.dot(mom_ref[...], jnp.concatenate([kept, kept], axis=0), preferred_element_type=f32)
        found = found[0:16] + found[16:32]
        for h in range(2):
            j = 2 * p + h
            e_stage[j] = found[:, h * LANES : (h + 1) * LANES].astype(jnp.bfloat16)

            @pl.when(j != z)
            def _():
                remote(e_stage.at[j], e_recv.at[z], e_ssem, e_rsem, dev(j, k, seq)).start()

            @pl.when(j == z)
            def _():
                local(e_stage.at[j], e_recv.at[z], e_rsem).start()

        return c

    lax.fori_loop(0, pairs, forward, 0)

    def inner(p, c):
        kept = z_keep[p]
        u_keep[...] = jnp.dot(
            toep_ref[...], jnp.concatenate([kept, kept], axis=0), preferred_element_type=f32
        )
        for h in range(2):
            j = 2 * p + h
            lanes = slice(h * LANES, (h + 1) * LANES)
            hs = [spread(h_all[t // share, j, t % share]) for t in range(TERMS)]
            skip = spread(h_all[TERMS // share, j, TERMS % share])
            for i in range(0, 2 * steps, 2):
                kept = z_keep[p, i * RUNS : (i + 2) * RUNS, lanes].astype(f32)
                for b in range(2):
                    row = (i + b) * RUNS
                    total = skip * kept[b * RUNS : (b + 1) * RUNS]
                    for t in range(TERMS):
                        total = total + hs[t] * u_keep[t * block + row : t * block + row + RUNS, lanes]
                    y_keep[j, row : row + RUNS, :] = total
        return c

    wait_bytes(h_col, a_rsem)

    def send_b(n, c):
        remote(h_col, h_all.at[seq], b_ssem, b_rsem, dev(z, k, (seq + n) % ns)).start()
        return c

    lax.fori_loop(1, ns, send_b, 0)
    local(h_col, h_all.at[seq], b_rsem).start()

    wait_bytes(e_recv, e_rsem)
    block_decay = jnp.exp(-decay * float(block))

    def along_z(zz, state):
        p_keep[zz] = state
        got = e_recv[zz].astype(f32)
        added = c_keep[0, 0] * got[0:1]
        for t in range(1, TERMS):
            added = added + c_keep[0, t] * got[t : t + 1]
        return block_decay * state + added

    t_stage[...] = lax.fori_loop(0, nz, along_z, jnp.zeros_like(decay)).astype(jnp.bfloat16)

    def send_t(ss, c):
        remote(t_stage, t_recv.at[seq], t_ssem.at[ss], t_rsem.at[seq], dev(z, k, ss)).start()
        return c

    lax.fori_loop(seq + 1, ns, send_t, 0)

    wait_bytes(h_all, b_rsem)
    ready((6, 7, 8))
    lax.fori_loop(0, nz // 4, inner, 0)

    seq_decay = jnp.exp(-decay * float(block * nz))

    def along_s(ss, state):
        wait_bytes(t_recv.at[ss], t_rsem.at[ss])
        return seq_decay * state + t_recv[ss].astype(f32)

    incoming = lax.fori_loop(0, seq, along_s, jnp.zeros_like(decay))

    def send_r(n, c):
        zz = (z + far_first(n)) % nz
        state = p_keep[zz] + jnp.exp(-decay * (zz * block).astype(f32)) * incoming
        for t in range(TERMS):
            r_flat[t : t + 1, :] = jnp.sum(c_keep[1, t] * state, axis=0, keepdims=True)
        r_stage[zz] = r_flat[...].astype(jnp.bfloat16)

        @pl.when(n < nz - 1)
        def _():
            remote(r_stage.at[zz], r_recv.at[z], r_ssem, r_rsem.at[z], dev(zz, k, seq)).start()

        @pl.when(n == nz - 1)
        def _():
            local(r_stage.at[zz], r_recv.at[z], r_rsem.at[z]).start()

        return c

    lax.fori_loop(0, nz, send_r, 0)
    lax.fori_loop(nz // 4, pairs, inner, 0)

    def finish(n, c):
        p = (z // 2 + far_first(pairs - 1 - n, pairs)) % (pairs)
        for h in range(2):
            j = 2 * p + h
            wait_bytes(r_recv.at[j], r_rsem.at[j])
        coef = jnp.concatenate([r_recv[2 * p], r_recv[2 * p + 1]], axis=1)
        none = jnp.zeros_like(coef)
        stacked = jnp.concatenate([coef, coef] + [none] * 6, axis=0)
        reached = jnp.dot(cross_ref[...], stacked, preferred_element_type=f32)
        for h in range(2):
            j = 2 * p + h
            for core in range(2):
                at = pl.ds(core * rows, 16)
                one, two = two_first(0, j, core)
                g_keep[j, at, :] = mend(g_keep[j, at, :], one, two)
            for i in range(0, 2 * steps, 2):
                gate = g_keep[j, i * RUNS : (i + 2) * RUNS, :].astype(f32)
                for b in range(2):
                    at = slice((i + b) * RUNS, (i + b + 1) * RUNS)
                    half, step = (i + b) // steps, (i + b) % steps
                    o_wide[h, run_rows(step, half * rows), :] = gate[b * RUNS : (b + 1) * RUNS] * (
                        y_keep[j, at, :] + reached[at, h * LANES : (h + 1) * LANES]
                    )
            o_keep[j] = o_wide[h].astype(jnp.bfloat16)
            local(o_keep.at[j, my_rows, :], out_ref.at[:, cols(j, k)], o_lsem).start()
            remote(
                o_keep.at[j, other_rows, :], out_ref.at[:, cols(j, k)], o_ssem, o_rsem, dev(z, other, seq)
            ).start()
        return c

    wait_bytes(g_out, g_rsem)
    lax.fori_loop(0, pairs, finish, 0)

    half = out_ref.at[:, pl.ds(0, nz * LANES)]
    wait_bytes(half, o_lsem)
    wait_bytes(half, o_ssem)
    wait_bytes(half, o_rsem)
    wait_bytes(z_out, z_ssem)
    wait_bytes(g_out, g_ssem)
    wait_bytes(edge_out, edge_ssem)
    wait_bytes(h_col.at[pl.ds(0, nz - 1)], a_ssem)
    wait_bytes(h_all.at[pl.ds(0, ns - 1)], b_ssem)
    wait_bytes(e_recv.at[pl.ds(0, nz - 1)], e_ssem)

    def sent_t(ss, c):
        wait_bytes(t_stage, t_ssem.at[ss])
        return c

    lax.fori_loop(seq + 1, ns, sent_t, 0)
    wait_bytes(r_recv.at[pl.ds(0, nz - 1)], r_ssem)

    @pl.when(sends_halo)
    def _():
        wait_bytes(halo_send, halo_ssem)


def per_device(nz, ns, features, short_taps, decay_rates, residues, skip_gain):
    streams, rows, width = features.shape
    modes = decay_rates.shape[0]
    block = 2 * rows
    pairs = nz // 2
    toeplitz, moments, cross = fixed_matrices(block)
    f32 = jnp.float32
    bf16 = jnp.bfloat16
    hbm = pl.BlockSpec(memory_space=pltpu.HBM)
    anywhere = pl.BlockSpec(memory_space=pl.ANY)
    dma = pltpu.SemaphoreType.DMA
    return pl.pallas_call(
        functools.partial(kernel, nz, ns),
        out_shape=jax.ShapeDtypeStruct((rows, width), jnp.bfloat16),
        in_specs=[hbm] * 8,
        out_specs=anywhere,
        scratch_shapes=[
            pltpu.VMEM(short_taps.shape, f32),
            pltpu.VMEM((modes, LANES), f32),
            pltpu.VMEM((modes, LANES), f32),
            pltpu.VMEM((1, LANES), f32),
            pltpu.VMEM((TERMS * block, 2 * block), bf16),
            pltpu.VMEM((32, 2 * block), bf16),
            pltpu.VMEM(cross.shape, bf16),
            pltpu.VMEM((pairs, streams, rows, 4 * LANES), bf16),
            pltpu.VMEM((2, nz, streams, 2, LANES), f32),
            pltpu.VMEM((nz, streams, 2, LANES), f32),
            pltpu.VMEM((nz, streams, 4, LANES), f32),
            pltpu.VMEM((2, nz, streams, 4, LANES), f32),
            pltpu.VMEM((pairs, rows, 2 * LANES), bf16),
            pltpu.VMEM((nz, rows, LANES), bf16),
            pltpu.VMEM((16, 1, LANES), f32),
            pltpu.VMEM((nz, 16 // ns, 1, LANES), f32),
            pltpu.VMEM((ns, nz, 16 // ns, 1, LANES), f32),
            pltpu.VMEM((2, TERMS, modes, LANES), f32),
            pltpu.VMEM((streams, rows, LANES), f32),
            pltpu.VMEM((pairs, block, 2 * LANES), bf16),
            pltpu.VMEM((nz, block, LANES), bf16),
            pltpu.VMEM((TERMS * block, 2 * LANES), f32),
            pltpu.VMEM((nz, block, LANES), f32),
            pltpu.VMEM((nz, 16, LANES), bf16),
            pltpu.VMEM((nz, 16, LANES), bf16),
            pltpu.VMEM((nz, modes, LANES), f32),
            pltpu.VMEM((modes, LANES), bf16),
            pltpu.VMEM((ns, modes, LANES), bf16),
            pltpu.VMEM((nz, 16, LANES), bf16),
            pltpu.VMEM((nz, 16, LANES), bf16),
            pltpu.VMEM((16, LANES), f32),
            pltpu.VMEM((2, block, LANES), f32),
            pltpu.VMEM((nz, block, LANES), bf16),
            dma((9,)),
            dma((pairs,)),
            dma,
            dma((pairs,)),
            dma,
            dma,
            dma,
            dma,
            dma,
            dma,
            dma,
            dma,
            dma,
            dma,
            dma,
            dma,
            dma((ns,)),
            dma((ns,)),
            dma,
            dma((nz,)),
            dma,
            dma,
            dma,
        ],
        compiler_params=pltpu.CompilerParams(
            collective_id=0, has_side_effects=True, vmem_limit_bytes=60 * 1024 * 1024
        ),
        cost_estimate=pl.CostEstimate(flops=40_000_000, bytes_accessed=2_200_000, transcendentals=0),
    )(short_taps, decay_rates, residues, skip_gain.reshape(1, -1), toeplitz, moments, cross, features)


def solution(mesh):
    nz, ns = mesh.shape["chan"] // 2, mesh.shape["seq"]
    placed = (P(None, ("seq", "chan"), None), P(), P(None, "chan"), P(None, "chan"), P("chan"))
    return jax.shard_map(
        functools.partial(per_device, nz, ns),
        mesh=mesh,
        in_specs=placed,
        out_specs=P(("seq", "chan"), None),
        check_vma=False,
    )
```

```python
import functools

import jax
import jax.numpy as jnp
import ml_dtypes
import numpy as np
from jax import lax
from jax.experimental import pallas as pl
from jax.experimental.pallas import tpu as pltpu
from jax.sharding import PartitionSpec as P

MESH = pl.DeviceIdType.MESH
LANES = 128
RUNS = 8
TERMS = 12


def fixed_matrices(block):
    half = block // 2
    steps = half // RUNS
    rows = np.arange(half)
    token = steps * (rows % RUNS) + rows // RUNS
    token = np.concatenate([token, half + token])

    def polys(lag):
        u = 2.0 * lag / block - 1.0
        out = [np.ones_like(u), u]
        while len(out) < TERMS:
            out.append(2.0 * u * out[-1] - out[-2])
        return np.stack(out)

    def parts(x):
        found = []
        for _ in range(3):
            found.append(x.astype(ml_dtypes.bfloat16))
            x = x - found[-1].astype(np.float64)
        return found

    lag = token[:, None] - token[None, :]
    inside = np.where(lag >= 0, polys(np.maximum(lag, 0).astype(np.float64)), 0.0)
    first, second, _ = parts(inside.reshape(TERMS * block, block))
    toeplitz = np.stack([first, second])

    end = np.zeros((16, block))
    end[:TERMS] = polys((block - 1 - token).astype(np.float64))
    first, second, third = parts(end)
    moments = np.stack([np.concatenate([first, third]), np.concatenate([second, 0 * third])])

    reach = np.zeros((block, 16))
    reach[:, :TERMS] = polys((token + 1).astype(np.float64)).T
    first, second, _ = parts(reach)
    none = 0 * first
    cross = np.concatenate([first, second] + [none] * 6, axis=1)
    return toeplitz, moments, cross


def one_minus_exp_neg(u):
    series = 1.0 - u * (1.0 / 8.0)
    for n in (7, 6, 5, 4, 3, 2):
        series = 1.0 - (u * (1.0 / n)) * series
    return jnp.where(u < 0.25, u * series, 1.0 - jnp.exp(-u))


def kernel(
    nz,
    ns,
    taps_hbm,
    decay_hbm,
    res_hbm,
    skip_hbm,
    toep_hbm,
    mom_hbm,
    cross_hbm,
    feat_ref,
    out_ref,
    taps_ref,
    decay_ref,
    res_ref,
    skip_ref,
    toep_ref,
    mom_ref,
    cross_ref,
    feats,
    halo_wide,
    halo_send,
    halo_recv,
    halo_past,
    edge_out,
    edges,
    z_out,
    g_out,
    h_src,
    h_col,
    h_all,
    c_keep,
    wide,
    z_keep,
    g_keep,
    u_keep,
    y_keep,
    e_stage,
    e_recv,
    p_keep,
    t_stage,
    t_recv,
    r_stage,
    r_recv,
    r_flat,
    o_wide,
    o_keep,
    arg_sem,
    local_sem,
    z_ssem,
    z_rsem,
    g_ssem,
    g_rsem,
    edge_ssem,
    edge_rsem,
    halo_ssem,
    halo_rsem,
    a_ssem,
    a_rsem,
    b_ssem,
    b_rsem,
    e_ssem,
    e_rsem,
    t_ssem,
    t_rsem,
    r_ssem,
    r_rsem,
    o_lsem,
    o_ssem,
    o_rsem,
):
    modes = decay_hbm.shape[0]
    share = 16 // ns
    rows = feat_ref.shape[1]
    block = 2 * rows
    steps = rows // RUNS
    pairs = nz // 2
    chan = lax.axis_index("chan")
    seq = lax.axis_index("seq")
    z = chan // 2
    k = chan % 2
    other = 1 - k
    position = seq * nz + z
    first = position == 0
    last = position == nz * ns - 1
    f32 = jnp.float32

    def dev(zz, kk, ss):
        return {"chan": zz * 2 + kk, "seq": ss}

    def remote(src, dst, ssem, rsem, device):
        return pltpu.make_async_remote_copy(
            src_ref=src, dst_ref=dst, send_sem=ssem, recv_sem=rsem, device_id=device, device_id_type=MESH
        )

    def local(src, dst, sem):
        return pltpu.make_async_copy(src, dst, sem)

    def wait_bytes(ref, sem):
        pltpu.make_async_copy(ref, ref, sem).wait()

    def far_first(n, of=nz):
        return (of // 2 + ((n + 1) // 2) * (1 - 2 * (n % 2))) % of

    def cols(j, kk):
        return pl.ds(pl.multiple_of((2 * j + kk) * LANES, LANES), LANES)

    my_rows = pl.ds(pl.multiple_of(k * rows, rows), rows)
    other_rows = pl.ds(pl.multiple_of(other * rows, rows), rows)

    barrier = pltpu.get_barrier_semaphore()

    def hello(device):
        pl.semaphore_signal(barrier, inc=1, device_id=device, device_id_type=MESH)

    for n in range(nz - 1):
        hello(dev((z + far_first(n)) % nz, k, seq))
    for n in range(1, ns):
        hello(dev(z, k, (seq + n) % ns))
    hello(dev(z, other, seq))
    before = position - 1 + nz * ns
    after = position + 1

    @pl.when(jnp.logical_not(first))
    def _():
        hello(dev(before % nz, 1, (before // nz) % ns))

    sends_halo = jnp.logical_and(k == 1, jnp.logical_not(last))

    wide_cols = 4 * LANES

    def chunk(p):
        at = pl.ds(pl.multiple_of(p * wide_cols, wide_cols), wide_cols)
        return local(feat_ref.at[:, :, at], feats.at[p], local_sem.at[p])

    def fetch(p, c):
        chunk(p).start()
        return c

    left, right = slice(0, block), slice(block, 2 * block)
    smalls = [
        (taps_hbm, taps_ref),
        (decay_hbm, decay_ref),
        (res_hbm, res_ref),
        (skip_hbm, skip_ref),
        (mom_hbm.at[0], mom_ref.at[:, left]),
        (mom_hbm.at[1], mom_ref.at[:, right]),
        (toep_hbm.at[0], toep_ref.at[:, left]),
        (toep_hbm.at[1], toep_ref.at[:, right]),
        (cross_hbm, cross_ref),
    ]

    def ready(numbers):
        for i in numbers:
            local(*smalls[i], arg_sem.at[i]).wait()

    local(*smalls[0], arg_sem.at[0]).start()
    lax.fori_loop(0, pairs, fetch, 0)
    for i, (src, dst) in enumerate(smalls[1:]):
        local(src, dst, arg_sem.at[1 + i]).start()
    ready((0,))

    row_id = lax.broadcasted_iota(jnp.int32, (RUNS, LANES), 0)

    def spread(row):
        return jnp.broadcast_to(row, (RUNS, LANES))

    def run_rows(i, base=0):
        return pl.ds(base + i, RUNS, stride=steps)

    def conv(p, c):
        chunk(p).wait()
        for h in range(2):
            j = 2 * p + h
            for mine in (True, False):
                kk = k if mine else other
                at = pl.ds(pl.multiple_of((2 * h + kk) * LANES, LANES), LANES)
                streams = []
                for q in range(3):
                    wide[q] = feats[p, q, :, at].astype(f32)
                    tap = [spread(taps_ref[q, t : t + 1, cols(j, kk)]) for t in range(3)]
                    own = [wide[q, run_rows(i), :] for i in range(steps)]
                    seen = [pltpu.roll(own[-2], 1, axis=0), pltpu.roll(own[-1], 1, axis=0)] + own
                    streams.append(
                        [tap[0] * seen[i + 2] + tap[1] * seen[i + 1] + tap[2] * seen[i] for i in range(steps)]
                    )
                    ends = [wide[q, 0:2, :], wide[q, rows - 2 : rows, :]]
                    kept = edges.at[k] if mine else edge_out
                    kept[j, q, 0:2, :] = ends[0]
                    kept[j, q, 2:4, :] = ends[1]
                    halo_wide[kk, pl.ds(j * 6 + 2 * q, 2), :] = ends[1]
                gate = jnp.concatenate(streams[0], axis=0).astype(jnp.bfloat16)
                product = jnp.concatenate([streams[1][i] * streams[2][i] for i in range(steps)], axis=0)
                product = product.astype(jnp.bfloat16)
                lanes = pl.ds(h * LANES, LANES)
                if mine:
                    z_keep[p, my_rows, lanes] = product
                    g_keep[j, my_rows, :] = gate
                else:
                    z_out[p, :, lanes] = product
                    g_out[j] = gate
        return c

    lax.fori_loop(0, pairs, conv, 0)
    halo_send[...] = halo_wide[...].astype(jnp.bfloat16)

    ready((1, 2, 3))
    decay = decay_ref[...]
    weight = res_ref[...] * jnp.sqrt(one_minus_exp_neg(2.0 * decay))
    half_a = decay * (block / 4.0)
    square = half_a * half_a
    lead = jnp.exp(-2.0 * half_a)
    for t in range(TERMS):
        total = jnp.ones_like(square)
        for i in range(10, 0, -1):
            total = 1.0 + square * (1.0 / (i * (i + t))) * total
        coef = lead * total * (1.0 if t == 0 else 2.0)
        lead = lead * half_a * (-1.0 / (t + 1))
        c_keep[0, t] = coef
        c_keep[1, t] = weight * coef
        h_src[t] = jnp.sum(weight * coef, axis=0, keepdims=True)
    for t in range(TERMS, 16):
        h_src[t] = skip_ref[...]
    r_flat[...] = jnp.zeros_like(r_flat)

    pl.semaphore_wait(barrier, (nz - 1) + (ns - 1) + 1 + 2 * sends_halo.astype(jnp.int32))

    @pl.when(sends_halo)
    def _():
        for kk in range(2):
            remote(
                halo_send.at[kk], halo_recv, halo_ssem, halo_rsem, dev(after % nz, kk, (after // nz) % ns)
            ).start()

    edge_copy = remote(edge_out, edges.at[k], edge_ssem, edge_rsem, dev(z, other, seq))
    edge_copy.start()

    def z_copy(p):
        return remote(z_out.at[p], z_keep.at[p, my_rows, :], z_ssem, z_rsem.at[p], dev(z, other, seq))

    def swap(n, c):
        z_copy((z // 2 + far_first(n, pairs)) % pairs).start()
        return c

    lax.fori_loop(0, pairs, swap, 0)

    my_rows_h = h_src.at[pl.ds(seq * share, share)]

    def send_a(n, c):
        remote(my_rows_h, h_col.at[z], a_ssem, a_rsem, dev((z + far_first(n)) % nz, k, seq)).start()
        return c

    lax.fori_loop(0, nz - 1, send_a, 0)
    local(my_rows_h, h_col.at[z], a_rsem).start()

    remote(g_out, g_keep.at[:, my_rows, :], g_ssem, g_rsem, dev(z, other, seq)).start()

    @pl.when(first)
    def _():
        halo_past[...] = jnp.zeros_like(halo_past)

    @pl.when(jnp.logical_not(first))
    def _():
        wait_bytes(halo_recv, halo_rsem)
        halo_past[...] = halo_recv[...].astype(f32)

    ready((4, 5))
    wait_bytes(edge_out, edge_rsem)

    def two_first(q, j, h):
        now = edges[h, j, q, 0:2, :]
        past = halo_past[pl.ds(j * 6 + 2 * q, 2), :] if h == 0 else edges[0, j, q, 2:4, :]
        tap = [taps_ref[q, t : t + 1, cols(j, k)] for t in range(3)]
        one = tap[0] * now[0:1] + tap[1] * past[1:2] + tap[2] * past[0:1]
        two = tap[0] * now[1:2] + tap[1] * now[0:1] + tap[2] * past[1:2]
        return one, two

    tile_row = lax.broadcasted_iota(jnp.int32, (16, LANES), 0)

    def mend(old, one, two):
        fresh = jnp.where(tile_row == 0, jnp.broadcast_to(one, (16, LANES)), old.astype(f32))
        fresh = jnp.where(tile_row == RUNS, jnp.broadcast_to(two, (16, LANES)), fresh)
        return fresh.astype(jnp.bfloat16)

    def forward(n, c):
        p = (z // 2 + far_first(n, pairs)) % pairs
        wait_bytes(z_out.at[p], z_rsem.at[p])
        for h in range(2):
            lanes = pl.ds(h * LANES, LANES)
            for core in range(2):
                at = pl.ds(core * rows, 16)
                second, third = two_first(1, 2 * p + h, core), two_first(2, 2 * p + h, core)
                z_keep[p, at, lanes] = mend(z_keep[p, at, lanes], second[0] * third[0], second[1] * third[1])
        kept = z_keep[p]
        found = jnp.dot(mom_ref[...], jnp.concatenate([kept, kept], axis=0), preferred_element_type=f32)
        found = found[0:16] + found[16:32]
        for h in range(2):
            j = 2 * p + h
            e_stage[j] = found[:, h * LANES : (h + 1) * LANES].astype(jnp.bfloat16)

            @pl.when(j != z)
            def _():
                remote(e_stage.at[j], e_recv.at[z], e_ssem, e_rsem, dev(j, k, seq)).start()

            @pl.when(j == z)
            def _():
                local(e_stage.at[j], e_recv.at[z], e_rsem).start()

        return c

    lax.fori_loop(0, pairs, forward, 0)

    def inner(p, c):
        kept = z_keep[p]
        u_keep[...] = jnp.dot(
            toep_ref[...], jnp.concatenate([kept, kept], axis=0), preferred_element_type=f32
        )
        for h in range(2):
            j = 2 * p + h
            lanes = slice(h * LANES, (h + 1) * LANES)
            hs = [spread(h_all[t // share, j, t % share]) for t in range(TERMS)]
            skip = spread(h_all[TERMS // share, j, TERMS % share])
            for i in range(0, 2 * steps, 2):
                kept = z_keep[p, i * RUNS : (i + 2) * RUNS, lanes].astype(f32)
                for b in range(2):
                    row = (i + b) * RUNS
                    total = skip * kept[b * RUNS : (b + 1) * RUNS]
                    for t in range(TERMS):
                        total = total + hs[t] * u_keep[t * block + row : t * block + row + RUNS, lanes]
                    y_keep[j, row : row + RUNS, :] = total
        return c

    wait_bytes(h_col, a_rsem)

    def send_b(n, c):
        remote(h_col, h_all.at[seq], b_ssem, b_rsem, dev(z, k, (seq + n) % ns)).start()
        return c

    lax.fori_loop(1, ns, send_b, 0)
    local(h_col, h_all.at[seq], b_rsem).start()

    wait_bytes(e_recv, e_rsem)
    block_decay = jnp.exp(-decay * float(block))

    def along_z(zz, state):
        p_keep[zz] = state
        got = e_recv[zz].astype(f32)
        added = c_keep[0, 0] * got[0:1]
        for t in range(1, TERMS):
            added = added + c_keep[0, t] * got[t : t + 1]
        return block_decay * state + added

    t_stage[...] = lax.fori_loop(0, nz, along_z, jnp.zeros_like(decay)).astype(jnp.bfloat16)

    def send_t(ss, c):
        remote(t_stage, t_recv.at[seq], t_ssem.at[ss], t_rsem.at[seq], dev(z, k, ss)).start()
        return c

    lax.fori_loop(seq + 1, ns, send_t, 0)

    wait_bytes(h_all, b_rsem)
    ready((6, 7, 8))
    early = jnp.where(seq == 0, 0, nz // 4)
    lax.fori_loop(0, early, inner, 0)

    seq_decay = jnp.exp(-decay * float(block * nz))

    def along_s(ss, state):
        wait_bytes(t_recv.at[ss], t_rsem.at[ss])
        return seq_decay * state + t_recv[ss].astype(f32)

    incoming = lax.fori_loop(0, seq, along_s, jnp.zeros_like(decay))

    def send_r(n, c):
        zz = (z + far_first(n)) % nz
        state = p_keep[zz] + jnp.exp(-decay * (zz * block).astype(f32)) * incoming
        for t in range(TERMS):
            r_flat[t : t + 1, :] = jnp.sum(c_keep[1, t] * state, axis=0, keepdims=True)
        r_stage[zz] = r_flat[...].astype(jnp.bfloat16)

        @pl.when(n < nz - 1)
        def _():
            remote(r_stage.at[zz], r_recv.at[z], r_ssem, r_rsem.at[z], dev(zz, k, seq)).start()

        @pl.when(n == nz - 1)
        def _():
            local(r_stage.at[zz], r_recv.at[z], r_rsem.at[z]).start()

        return c

    lax.fori_loop(0, nz, send_r, 0)
    lax.fori_loop(early, pairs, inner, 0)

    def finish(n, c):
        p = (z // 2 + far_first(pairs - 1 - n, pairs)) % (pairs)
        for h in range(2):
            j = 2 * p + h
            wait_bytes(r_recv.at[j], r_rsem.at[j])
        coef = jnp.concatenate([r_recv[2 * p], r_recv[2 * p + 1]], axis=1)
        none = jnp.zeros_like(coef)
        stacked = jnp.concatenate([coef, coef] + [none] * 6, axis=0)
        reached = jnp.dot(cross_ref[...], stacked, preferred_element_type=f32)
        for h in range(2):
            j = 2 * p + h
            for core in range(2):
                at = pl.ds(core * rows, 16)
                one, two = two_first(0, j, core)
                g_keep[j, at, :] = mend(g_keep[j, at, :], one, two)
            for i in range(0, 2 * steps, 2):
                gate = g_keep[j, i * RUNS : (i + 2) * RUNS, :].astype(f32)
                for b in range(2):
                    at = slice((i + b) * RUNS, (i + b + 1) * RUNS)
                    half, step = (i + b) // steps, (i + b) % steps
                    o_wide[h, run_rows(step, half * rows), :] = gate[b * RUNS : (b + 1) * RUNS] * (
                        y_keep[j, at, :] + reached[at, h * LANES : (h + 1) * LANES]
                    )
            o_keep[j] = o_wide[h].astype(jnp.bfloat16)
            local(o_keep.at[j, my_rows, :], out_ref.at[:, cols(j, k)], o_lsem).start()
            remote(
                o_keep.at[j, other_rows, :], out_ref.at[:, cols(j, k)], o_ssem, o_rsem, dev(z, other, seq)
            ).start()
        return c

    wait_bytes(g_out, g_rsem)
    lax.fori_loop(0, pairs, finish, 0)

    half = out_ref.at[:, pl.ds(0, nz * LANES)]
    wait_bytes(half, o_lsem)
    wait_bytes(half, o_ssem)
    wait_bytes(half, o_rsem)
    wait_bytes(z_out, z_ssem)
    wait_bytes(g_out, g_ssem)
    wait_bytes(edge_out, edge_ssem)
    wait_bytes(h_col.at[pl.ds(0, nz - 1)], a_ssem)
    wait_bytes(h_all.at[pl.ds(0, ns - 1)], b_ssem)
    wait_bytes(e_recv.at[pl.ds(0, nz - 1)], e_ssem)

    def sent_t(ss, c):
        wait_bytes(t_stage, t_ssem.at[ss])
        return c

    lax.fori_loop(seq + 1, ns, sent_t, 0)
    wait_bytes(r_recv.at[pl.ds(0, nz - 1)], r_ssem)

    @pl.when(sends_halo)
    def _():
        wait_bytes(halo_send, halo_ssem)


def per_device(nz, ns, features, short_taps, decay_rates, residues, skip_gain):
    streams, rows, width = features.shape
    modes = decay_rates.shape[0]
    block = 2 * rows
    pairs = nz // 2
    toeplitz, moments, cross = fixed_matrices(block)
    f32 = jnp.float32
    bf16 = jnp.bfloat16
    hbm = pl.BlockSpec(memory_space=pltpu.HBM)
    anywhere = pl.BlockSpec(memory_space=pl.ANY)
    dma = pltpu.SemaphoreType.DMA
    return pl.pallas_call(
        functools.partial(kernel, nz, ns),
        out_shape=jax.ShapeDtypeStruct((rows, width), jnp.bfloat16),
        in_specs=[hbm] * 8,
        out_specs=anywhere,
        scratch_shapes=[
            pltpu.VMEM(short_taps.shape, f32),
            pltpu.VMEM((modes, LANES), f32),
            pltpu.VMEM((modes, LANES), f32),
            pltpu.VMEM((1, LANES), f32),
            pltpu.VMEM((TERMS * block, 2 * block), bf16),
            pltpu.VMEM((32, 2 * block), bf16),
            pltpu.VMEM(cross.shape, bf16),
            pltpu.VMEM((pairs, streams, rows, 4 * LANES), bf16),
            pltpu.VMEM((2, nz * 2 * streams, LANES), f32),
            pltpu.VMEM((2, nz * 2 * streams, LANES), bf16),
            pltpu.VMEM((nz * 2 * streams, LANES), bf16),
            pltpu.VMEM((nz * 2 * streams, LANES), f32),
            pltpu.VMEM((nz, streams, 4, LANES), f32),
            pltpu.VMEM((2, nz, streams, 4, LANES), f32),
            pltpu.VMEM((pairs, rows, 2 * LANES), bf16),
            pltpu.VMEM((nz, rows, LANES), bf16),
            pltpu.VMEM((16, 1, LANES), f32),
            pltpu.VMEM((nz, 16 // ns, 1, LANES), f32),
            pltpu.VMEM((ns, nz, 16 // ns, 1, LANES), f32),
            pltpu.VMEM((2, TERMS, modes, LANES), f32),
            pltpu.VMEM((streams, rows, LANES), f32),
            pltpu.VMEM((pairs, block, 2 * LANES), bf16),
            pltpu.VMEM((nz, block, LANES), bf16),
            pltpu.VMEM((TERMS * block, 2 * LANES), f32),
            pltpu.VMEM((nz, block, LANES), f32),
            pltpu.VMEM((nz, 16, LANES), bf16),
            pltpu.VMEM((nz, 16, LANES), bf16),
            pltpu.VMEM((nz, modes, LANES), f32),
            pltpu.VMEM((modes, LANES), bf16),
            pltpu.VMEM((ns, modes, LANES), bf16),
            pltpu.VMEM((nz, 16, LANES), bf16),
            pltpu.VMEM((nz, 16, LANES), bf16),
            pltpu.VMEM((16, LANES), f32),
            pltpu.VMEM((2, block, LANES), f32),
            pltpu.VMEM((nz, block, LANES), bf16),
            dma((9,)),
            dma((pairs,)),
            dma,
            dma((pairs,)),
            dma,
            dma,
            dma,
            dma,
            dma,
            dma,
            dma,
            dma,
            dma,
            dma,
            dma,
            dma,
            dma((ns,)),
            dma((ns,)),
            dma,
            dma((nz,)),
            dma,
            dma,
            dma,
        ],
        compiler_params=pltpu.CompilerParams(
            collective_id=0, has_side_effects=True, vmem_limit_bytes=60 * 1024 * 1024
        ),
        cost_estimate=pl.CostEstimate(flops=40_000_000, bytes_accessed=2_200_000, transcendentals=0),
    )(short_taps, decay_rates, residues, skip_gain.reshape(1, -1), toeplitz, moments, cross, features)


def solution(mesh):
    nz, ns = mesh.shape["chan"] // 2, mesh.shape["seq"]
    placed = (P(None, ("seq", "chan"), None), P(), P(None, "chan"), P(None, "chan"), P("chan"))
    return jax.shard_map(
        functools.partial(per_device, nz, ns),
        mesh=mesh,
        in_specs=placed,
        out_specs=P(("seq", "chan"), None),
        check_vma=False,
    )
```

```python
import functools

import jax
import jax.numpy as jnp
import ml_dtypes
import numpy as np
from jax import lax
from jax.experimental import pallas as pl
from jax.experimental.pallas import tpu as pltpu
from jax.sharding import PartitionSpec as P

MESH = pl.DeviceIdType.MESH
LANES = 128
RUNS = 8
TERMS = 12


def fixed_matrices(block):
    half = block // 2
    steps = half // RUNS
    rows = np.arange(half)
    token = steps * (rows % RUNS) + rows // RUNS
    token = np.concatenate([token, half + token])

    def polys(lag):
        u = 2.0 * lag / block - 1.0
        out = [np.ones_like(u), u]
        while len(out) < TERMS:
            out.append(2.0 * u * out[-1] - out[-2])
        return np.stack(out)

    def parts(x):
        found = []
        for _ in range(3):
            found.append(x.astype(ml_dtypes.bfloat16))
            x = x - found[-1].astype(np.float64)
        return found

    lag = token[:, None] - token[None, :]
    inside = np.where(lag >= 0, polys(np.maximum(lag, 0).astype(np.float64)), 0.0)
    first, second, _ = parts(inside.reshape(TERMS * block, block))
    toeplitz = np.stack([first, second])

    end = np.zeros((16, block))
    end[:TERMS] = polys((block - 1 - token).astype(np.float64))
    first, second, third = parts(end)
    moments = np.stack([np.concatenate([first, third]), np.concatenate([second, 0 * third])])

    reach = np.zeros((block, 16))
    reach[:, :TERMS] = polys((token + 1).astype(np.float64)).T
    first, second, _ = parts(reach)
    none = 0 * first
    cross = np.concatenate([first, second] + [none] * 6, axis=1)
    return toeplitz, moments, cross


def one_minus_exp_neg(u):
    series = 1.0 - u * (1.0 / 8.0)
    for n in (7, 6, 5, 4, 3, 2):
        series = 1.0 - (u * (1.0 / n)) * series
    return jnp.where(u < 0.25, u * series, 1.0 - jnp.exp(-u))


def kernel(
    nz,
    ns,
    taps_hbm,
    decay_hbm,
    res_hbm,
    skip_hbm,
    toep_hbm,
    mom_hbm,
    cross_hbm,
    feat_ref,
    out_ref,
    taps_ref,
    decay_ref,
    res_ref,
    skip_ref,
    toep_ref,
    mom_ref,
    cross_ref,
    feats,
    halo_wide,
    halo_send,
    halo_recv,
    halo_past,
    edge_out,
    edges,
    z_out,
    g_out,
    h_src,
    h_col,
    h_all,
    c_keep,
    wide,
    z_keep,
    g_keep,
    u_keep,
    y_keep,
    e_stage,
    e_recv,
    p_keep,
    t_stage,
    t_recv,
    r_stage,
    r_recv,
    r_flat,
    o_wide,
    o_keep,
    arg_sem,
    local_sem,
    z_ssem,
    z_rsem,
    g_ssem,
    g_rsem,
    edge_ssem,
    edge_rsem,
    halo_ssem,
    halo_rsem,
    a_ssem,
    a_rsem,
    b_ssem,
    b_rsem,
    e_ssem,
    e_rsem,
    t_ssem,
    t_rsem,
    r_ssem,
    r_rsem,
    o_lsem,
    o_ssem,
    o_rsem,
):
    modes = decay_hbm.shape[0]
    share = 16 // ns
    rows = feat_ref.shape[1]
    block = 2 * rows
    steps = rows // RUNS
    pairs = nz // 2
    chan = lax.axis_index("chan")
    seq = lax.axis_index("seq")
    z = chan // 2
    k = chan % 2
    other = 1 - k
    position = seq * nz + z
    first = position == 0
    last = position == nz * ns - 1
    f32 = jnp.float32

    def dev(zz, kk, ss):
        return {"chan": zz * 2 + kk, "seq": ss}

    def remote(src, dst, ssem, rsem, device):
        return pltpu.make_async_remote_copy(
            src_ref=src, dst_ref=dst, send_sem=ssem, recv_sem=rsem, device_id=device, device_id_type=MESH
        )

    def local(src, dst, sem):
        return pltpu.make_async_copy(src, dst, sem)

    def wait_bytes(ref, sem):
        pltpu.make_async_copy(ref, ref, sem).wait()

    def far_first(n, of=nz):
        return (of // 2 + ((n + 1) // 2) * (1 - 2 * (n % 2))) % of

    def cols(j, kk):
        return pl.ds(pl.multiple_of((2 * j + kk) * LANES, LANES), LANES)

    my_rows = pl.ds(pl.multiple_of(k * rows, rows), rows)
    other_rows = pl.ds(pl.multiple_of(other * rows, rows), rows)

    barrier = pltpu.get_barrier_semaphore()

    def hello(device):
        pl.semaphore_signal(barrier, inc=1, device_id=device, device_id_type=MESH)

    for n in range(nz - 1):
        hello(dev((z + far_first(n)) % nz, k, seq))
    for n in range(1, ns):
        hello(dev(z, k, (seq + n) % ns))
    hello(dev(z, other, seq))
    before = position - 1 + nz * ns
    after = position + 1

    @pl.when(jnp.logical_not(first))
    def _():
        hello(dev(before % nz, 1, (before // nz) % ns))

    sends_halo = jnp.logical_and(k == 1, jnp.logical_not(last))

    wide_cols = 4 * LANES

    def chunk(p):
        at = pl.ds(pl.multiple_of(p * wide_cols, wide_cols), wide_cols)
        return local(feat_ref.at[:, :, at], feats.at[p], local_sem.at[p])

    def fetch(p, c):
        chunk(p).start()
        return c

    left, right = slice(0, block), slice(block, 2 * block)
    smalls = [
        (taps_hbm, taps_ref),
        (decay_hbm, decay_ref),
        (res_hbm, res_ref),
        (skip_hbm, skip_ref),
        (mom_hbm.at[0], mom_ref.at[:, left]),
        (mom_hbm.at[1], mom_ref.at[:, right]),
        (toep_hbm.at[0], toep_ref.at[:, left]),
        (toep_hbm.at[1], toep_ref.at[:, right]),
        (cross_hbm, cross_ref),
    ]

    def ready(numbers):
        for i in numbers:
            local(*smalls[i], arg_sem.at[i]).wait()

    local(*smalls[0], arg_sem.at[0]).start()
    lax.fori_loop(0, pairs, fetch, 0)
    for i, (src, dst) in enumerate(smalls[1:]):
        local(src, dst, arg_sem.at[1 + i]).start()
    ready((0,))

    row_id = lax.broadcasted_iota(jnp.int32, (RUNS, LANES), 0)

    def spread(row):
        return jnp.broadcast_to(row, (RUNS, LANES))

    def run_rows(i, base=0):
        return pl.ds(base + i, RUNS, stride=steps)

    def conv(p, c):
        chunk(p).wait()
        for h in range(2):
            j = 2 * p + h
            for mine in (True, False):
                kk = k if mine else other
                at = pl.ds(pl.multiple_of((2 * h + kk) * LANES, LANES), LANES)
                streams = []
                for q in range(3):
                    wide[q] = feats[p, q, :, at].astype(f32)
                    tap = [spread(taps_ref[q, t : t + 1, cols(j, kk)]) for t in range(3)]
                    own = [wide[q, run_rows(i), :] for i in range(steps)]
                    seen = [pltpu.roll(own[-2], 1, axis=0), pltpu.roll(own[-1], 1, axis=0)] + own
                    streams.append(
                        [tap[0] * seen[i + 2] + tap[1] * seen[i + 1] + tap[2] * seen[i] for i in range(steps)]
                    )
                    ends = [wide[q, 0:2, :], wide[q, rows - 2 : rows, :]]
                    kept = edges.at[k] if mine else edge_out
                    kept[j, q, 0:2, :] = ends[0]
                    kept[j, q, 2:4, :] = ends[1]
                    halo_wide[kk, pl.ds(j * 6 + 2 * q, 2), :] = ends[1]
                gate = jnp.concatenate(streams[0], axis=0).astype(jnp.bfloat16)
                product = jnp.concatenate([streams[1][i] * streams[2][i] for i in range(steps)], axis=0)
                product = product.astype(jnp.bfloat16)
                lanes = pl.ds(h * LANES, LANES)
                if mine:
                    z_keep[p, my_rows, lanes] = product
                    g_keep[j, my_rows, :] = gate
                else:
                    z_out[p, :, lanes] = product
                    g_out[j] = gate
        return c

    lax.fori_loop(0, pairs, conv, 0)
    halo_send[...] = halo_wide[...].astype(jnp.bfloat16)

    ready((1, 2, 3))
    decay = decay_ref[...]
    weight = res_ref[...] * jnp.sqrt(one_minus_exp_neg(2.0 * decay))
    half_a = decay * (block / 4.0)
    square = half_a * half_a
    lead = jnp.exp(-2.0 * half_a)
    for t in range(TERMS):
        total = jnp.ones_like(square)
        for i in range(10, 0, -1):
            total = 1.0 + square * (1.0 / (i * (i + t))) * total
        coef = lead * total * (1.0 if t == 0 else 2.0)
        lead = lead * half_a * (-1.0 / (t + 1))
        c_keep[0, t] = coef
        c_keep[1, t] = weight * coef
        h_src[t] = jnp.sum(weight * coef, axis=0, keepdims=True)
    for t in range(TERMS, 16):
        h_src[t] = skip_ref[...]
    r_flat[...] = jnp.zeros_like(r_flat)

    pl.semaphore_wait(barrier, (nz - 1) + (ns - 1) + 1 + 2 * sends_halo.astype(jnp.int32))

    @pl.when(sends_halo)
    def _():
        for kk in range(2):
            remote(
                halo_send.at[kk], halo_recv, halo_ssem, halo_rsem, dev(after % nz, kk, (after // nz) % ns)
            ).start()

    edge_copy = remote(edge_out, edges.at[k], edge_ssem, edge_rsem, dev(z, other, seq))
    edge_copy.start()

    def z_copy(p):
        return remote(z_out.at[p], z_keep.at[p, my_rows, :], z_ssem, z_rsem.at[p], dev(z, other, seq))

    def swap(n, c):
        z_copy((z // 2 + far_first(n, pairs)) % pairs).start()
        return c

    lax.fori_loop(0, pairs, swap, 0)

    my_rows_h = h_src.at[pl.ds(seq * share, share)]

    def send_a(n, c):
        remote(my_rows_h, h_col.at[z], a_ssem, a_rsem, dev((z + far_first(n)) % nz, k, seq)).start()
        return c

    lax.fori_loop(0, nz - 1, send_a, 0)
    local(my_rows_h, h_col.at[z], a_rsem).start()

    remote(g_out, g_keep.at[:, my_rows, :], g_ssem, g_rsem, dev(z, other, seq)).start()

    @pl.when(first)
    def _():
        halo_past[...] = jnp.zeros_like(halo_past)

    @pl.when(jnp.logical_not(first))
    def _():
        wait_bytes(halo_recv, halo_rsem)
        halo_past[...] = halo_recv[...].astype(f32)

    ready((4, 5))
    wait_bytes(edge_out, edge_rsem)

    def two_first(q, j, h):
        now = edges[h, j, q, 0:2, :]
        past = halo_past[pl.ds(j * 6 + 2 * q, 2), :] if h == 0 else edges[0, j, q, 2:4, :]
        tap = [taps_ref[q, t : t + 1, cols(j, k)] for t in range(3)]
        one = tap[0] * now[0:1] + tap[1] * past[1:2] + tap[2] * past[0:1]
        two = tap[0] * now[1:2] + tap[1] * now[0:1] + tap[2] * past[1:2]
        return one, two

    tile_row = lax.broadcasted_iota(jnp.int32, (16, LANES), 0)

    def mend(old, one, two):
        fresh = jnp.where(tile_row == 0, jnp.broadcast_to(one, (16, LANES)), old.astype(f32))
        fresh = jnp.where(tile_row == RUNS, jnp.broadcast_to(two, (16, LANES)), fresh)
        return fresh.astype(jnp.bfloat16)

    def forward(n, c):
        p = (z // 2 + far_first(n, pairs)) % pairs
        wait_bytes(z_out.at[p], z_rsem.at[p])
        for h in range(2):
            lanes = pl.ds(h * LANES, LANES)
            for core in range(2):
                at = pl.ds(core * rows, 16)
                second, third = two_first(1, 2 * p + h, core), two_first(2, 2 * p + h, core)
                z_keep[p, at, lanes] = mend(z_keep[p, at, lanes], second[0] * third[0], second[1] * third[1])
        kept = z_keep[p]
        found = jnp.dot(mom_ref[...], jnp.concatenate([kept, kept], axis=0), preferred_element_type=f32)
        found = found[0:16] + found[16:32]
        for h in range(2):
            j = 2 * p + h
            e_stage[j] = found[:, h * LANES : (h + 1) * LANES].astype(jnp.bfloat16)

            @pl.when(j != z)
            def _():
                remote(e_stage.at[j], e_recv.at[z], e_ssem, e_rsem, dev(j, k, seq)).start()

            @pl.when(j == z)
            def _():
                local(e_stage.at[j], e_recv.at[z], e_rsem).start()

        return c

    lax.fori_loop(0, pairs, forward, 0)

    def inner(p, c):
        kept = z_keep[p]
        u_keep[...] = jnp.dot(
            toep_ref[...], jnp.concatenate([kept, kept], axis=0), preferred_element_type=f32
        )
        for h in range(2):
            j = 2 * p + h
            lanes = slice(h * LANES, (h + 1) * LANES)
            hs = [spread(h_all[t // share, j, t % share]) for t in range(TERMS)]
            skip = spread(h_all[TERMS // share, j, TERMS % share])
            for i in range(0, 2 * steps, 2):
                kept = z_keep[p, i * RUNS : (i + 2) * RUNS, lanes].astype(f32)
                for b in range(2):
                    row = (i + b) * RUNS
                    total = skip * kept[b * RUNS : (b + 1) * RUNS]
                    for t in range(TERMS):
                        total = total + hs[t] * u_keep[t * block + row : t * block + row + RUNS, lanes]
                    y_keep[j, row : row + RUNS, :] = total
        return c

    wait_bytes(h_col, a_rsem)

    def send_b(n, c):
        remote(h_col, h_all.at[seq], b_ssem, b_rsem, dev(z, k, (seq + n) % ns)).start()
        return c

    lax.fori_loop(1, ns, send_b, 0)
    local(h_col, h_all.at[seq], b_rsem).start()

    wait_bytes(e_recv, e_rsem)
    block_decay = jnp.exp(-decay * float(block))

    def along_z(zz, state):
        p_keep[zz] = state
        got = e_recv[zz].astype(f32)
        added = c_keep[0, 0] * got[0:1]
        for t in range(1, TERMS):
            added = added + c_keep[0, t] * got[t : t + 1]
        return block_decay * state + added

    t_stage[...] = lax.fori_loop(0, nz, along_z, jnp.zeros_like(decay)).astype(jnp.bfloat16)

    def send_t(ss, c):
        remote(t_stage, t_recv.at[seq], t_ssem.at[ss], t_rsem.at[seq], dev(z, k, ss)).start()
        return c

    lax.fori_loop(seq + 1, ns, send_t, 0)

    seq_decay = jnp.exp(-decay * float(block * nz))

    def along_s(ss, state):
        wait_bytes(t_recv.at[ss], t_rsem.at[ss])
        return seq_decay * state + t_recv[ss].astype(f32)

    incoming = lax.fori_loop(0, seq, along_s, jnp.zeros_like(decay))

    def send_r(n, c):
        zz = (z + far_first(n)) % nz
        state = p_keep[zz] + jnp.exp(-decay * (zz * block).astype(f32)) * incoming
        for t in range(TERMS):
            r_flat[t : t + 1, :] = jnp.sum(c_keep[1, t] * state, axis=0, keepdims=True)
        r_stage[zz] = r_flat[...].astype(jnp.bfloat16)

        @pl.when(n < nz - 1)
        def _():
            remote(r_stage.at[zz], r_recv.at[z], r_ssem, r_rsem.at[z], dev(zz, k, seq)).start()

        @pl.when(n == nz - 1)
        def _():
            local(r_stage.at[zz], r_recv.at[z], r_rsem.at[z]).start()

        return c

    lax.fori_loop(0, nz, send_r, 0)
    wait_bytes(h_all, b_rsem)
    ready((6, 7, 8))
    lax.fori_loop(0, pairs, inner, 0)

    def finish(n, c):
        p = (z // 2 + far_first(pairs - 1 - n, pairs)) % (pairs)
        for h in range(2):
            j = 2 * p + h
            wait_bytes(r_recv.at[j], r_rsem.at[j])
        coef = jnp.concatenate([r_recv[2 * p], r_recv[2 * p + 1]], axis=1)
        none = jnp.zeros_like(coef)
        stacked = jnp.concatenate([coef, coef] + [none] * 6, axis=0)
        reached = jnp.dot(cross_ref[...], stacked, preferred_element_type=f32)
        for h in range(2):
            j = 2 * p + h
            for core in range(2):
                at = pl.ds(core * rows, 16)
                one, two = two_first(0, j, core)
                g_keep[j, at, :] = mend(g_keep[j, at, :], one, two)
            for i in range(0, 2 * steps, 2):
                gate = g_keep[j, i * RUNS : (i + 2) * RUNS, :].astype(f32)
                for b in range(2):
                    at = slice((i + b) * RUNS, (i + b + 1) * RUNS)
                    half, step = (i + b) // steps, (i + b) % steps
                    o_wide[h, run_rows(step, half * rows), :] = gate[b * RUNS : (b + 1) * RUNS] * (
                        y_keep[j, at, :] + reached[at, h * LANES : (h + 1) * LANES]
                    )
            o_keep[j] = o_wide[h].astype(jnp.bfloat16)
            local(o_keep.at[j, my_rows, :], out_ref.at[:, cols(j, k)], o_lsem).start()
            remote(
                o_keep.at[j, other_rows, :], out_ref.at[:, cols(j, k)], o_ssem, o_rsem, dev(z, other, seq)
            ).start()
        return c

    wait_bytes(g_out, g_rsem)
    lax.fori_loop(0, pairs, finish, 0)

    half = out_ref.at[:, pl.ds(0, nz * LANES)]
    wait_bytes(half, o_lsem)
    wait_bytes(half, o_ssem)
    wait_bytes(half, o_rsem)
    wait_bytes(z_out, z_ssem)
    wait_bytes(g_out, g_ssem)
    wait_bytes(edge_out, edge_ssem)
    wait_bytes(h_col.at[pl.ds(0, nz - 1)], a_ssem)
    wait_bytes(h_all.at[pl.ds(0, ns - 1)], b_ssem)
    wait_bytes(e_recv.at[pl.ds(0, nz - 1)], e_ssem)

    def sent_t(ss, c):
        wait_bytes(t_stage, t_ssem.at[ss])
        return c

    lax.fori_loop(seq + 1, ns, sent_t, 0)
    wait_bytes(r_recv.at[pl.ds(0, nz - 1)], r_ssem)

    @pl.when(sends_halo)
    def _():
        wait_bytes(halo_send, halo_ssem)


def per_device(nz, ns, features, short_taps, decay_rates, residues, skip_gain):
    streams, rows, width = features.shape
    modes = decay_rates.shape[0]
    block = 2 * rows
    pairs = nz // 2
    toeplitz, moments, cross = fixed_matrices(block)
    f32 = jnp.float32
    bf16 = jnp.bfloat16
    hbm = pl.BlockSpec(memory_space=pltpu.HBM)
    anywhere = pl.BlockSpec(memory_space=pl.ANY)
    dma = pltpu.SemaphoreType.DMA
    return pl.pallas_call(
        functools.partial(kernel, nz, ns),
        out_shape=jax.ShapeDtypeStruct((rows, width), jnp.bfloat16),
        in_specs=[hbm] * 8,
        out_specs=anywhere,
        scratch_shapes=[
            pltpu.VMEM(short_taps.shape, f32),
            pltpu.VMEM((modes, LANES), f32),
            pltpu.VMEM((modes, LANES), f32),
            pltpu.VMEM((1, LANES), f32),
            pltpu.VMEM((TERMS * block, 2 * block), bf16),
            pltpu.VMEM((32, 2 * block), bf16),
            pltpu.VMEM(cross.shape, bf16),
            pltpu.VMEM((pairs, streams, rows, 4 * LANES), bf16),
            pltpu.VMEM((2, nz * 2 * streams, LANES), f32),
            pltpu.VMEM((2, nz * 2 * streams, LANES), bf16),
            pltpu.VMEM((nz * 2 * streams, LANES), bf16),
            pltpu.VMEM((nz * 2 * streams, LANES), f32),
            pltpu.VMEM((nz, streams, 4, LANES), f32),
            pltpu.VMEM((2, nz, streams, 4, LANES), f32),
            pltpu.VMEM((pairs, rows, 2 * LANES), bf16),
            pltpu.VMEM((nz, rows, LANES), bf16),
            pltpu.VMEM((16, 1, LANES), f32),
            pltpu.VMEM((nz, 16 // ns, 1, LANES), f32),
            pltpu.VMEM((ns, nz, 16 // ns, 1, LANES), f32),
            pltpu.VMEM((2, TERMS, modes, LANES), f32),
            pltpu.VMEM((streams, rows, LANES), f32),
            pltpu.VMEM((pairs, block, 2 * LANES), bf16),
            pltpu.VMEM((nz, block, LANES), bf16),
            pltpu.VMEM((TERMS * block, 2 * LANES), f32),
            pltpu.VMEM((nz, block, LANES), f32),
            pltpu.VMEM((nz, 16, LANES), bf16),
            pltpu.VMEM((nz, 16, LANES), bf16),
            pltpu.VMEM((nz, modes, LANES), f32),
            pltpu.VMEM((modes, LANES), bf16),
            pltpu.VMEM((ns, modes, LANES), bf16),
            pltpu.VMEM((nz, 16, LANES), bf16),
            pltpu.VMEM((nz, 16, LANES), bf16),
            pltpu.VMEM((16, LANES), f32),
            pltpu.VMEM((2, block, LANES), f32),
            pltpu.VMEM((nz, block, LANES), bf16),
            dma((9,)),
            dma((pairs,)),
            dma,
            dma((pairs,)),
            dma,
            dma,
            dma,
            dma,
            dma,
            dma,
            dma,
            dma,
            dma,
            dma,
            dma,
            dma,
            dma((ns,)),
            dma((ns,)),
            dma,
            dma((nz,)),
            dma,
            dma,
            dma,
        ],
        compiler_params=pltpu.CompilerParams(
            collective_id=0, has_side_effects=True, vmem_limit_bytes=60 * 1024 * 1024
        ),
        cost_estimate=pl.CostEstimate(flops=40_000_000, bytes_accessed=2_200_000, transcendentals=0),
    )(short_taps, decay_rates, residues, skip_gain.reshape(1, -1), toeplitz, moments, cross, features)


def solution(mesh):
    nz, ns = mesh.shape["chan"] // 2, mesh.shape["seq"]
    placed = (P(None, ("seq", "chan"), None), P(), P(None, "chan"), P(None, "chan"), P("chan"))
    return jax.shard_map(
        functools.partial(per_device, nz, ns),
        mesh=mesh,
        in_specs=placed,
        out_specs=P(("seq", "chan"), None),
        check_vma=False,
    )
```

```python
import functools

import jax
import jax.numpy as jnp
import ml_dtypes
import numpy as np
from jax import lax
from jax.experimental import pallas as pl
from jax.experimental.pallas import tpu as pltpu
from jax.sharding import PartitionSpec as P

MESH = pl.DeviceIdType.MESH
LANES = 128
RUNS = 8
TERMS = 12


def fixed_matrices(block):
    half = block // 2
    steps = half // RUNS
    rows = np.arange(half)
    token = steps * (rows % RUNS) + rows // RUNS
    token = np.concatenate([token, half + token])

    def polys(lag):
        u = 2.0 * lag / block - 1.0
        out = [np.ones_like(u), u]
        while len(out) < TERMS:
            out.append(2.0 * u * out[-1] - out[-2])
        return np.stack(out)

    def parts(x):
        found = []
        for _ in range(3):
            found.append(x.astype(ml_dtypes.bfloat16))
            x = x - found[-1].astype(np.float64)
        return found

    lag = token[:, None] - token[None, :]
    inside = np.where(lag >= 0, polys(np.maximum(lag, 0).astype(np.float64)), 0.0)
    first, second, _ = parts(inside.reshape(TERMS * block, block))
    toeplitz = np.stack([first, second])

    end = np.zeros((16, block))
    end[:TERMS] = polys((block - 1 - token).astype(np.float64))
    first, second, third = parts(end)
    moments = np.stack([np.concatenate([first, third]), np.concatenate([second, 0 * third])])

    reach = np.zeros((block, 16))
    reach[:, :TERMS] = polys((token + 1).astype(np.float64)).T
    first, second, _ = parts(reach)
    none = 0 * first
    cross = np.concatenate([first, second] + [none] * 6, axis=1)
    return toeplitz, moments, cross


def one_minus_exp_neg(u):
    series = 1.0 - u * (1.0 / 8.0)
    for n in (7, 6, 5, 4, 3, 2):
        series = 1.0 - (u * (1.0 / n)) * series
    return jnp.where(u < 0.25, u * series, 1.0 - jnp.exp(-u))


def kernel(
    nz,
    ns,
    taps_hbm,
    decay_hbm,
    res_hbm,
    skip_hbm,
    toep_hbm,
    mom_hbm,
    cross_hbm,
    feat_ref,
    out_ref,
    taps_ref,
    decay_ref,
    res_ref,
    skip_ref,
    toep_ref,
    mom_ref,
    cross_ref,
    feats,
    halo_wide,
    halo_send,
    halo_recv,
    halo_past,
    edge_out,
    edges,
    z_out,
    g_out,
    h_src,
    h_col,
    h_all,
    c_keep,
    wide,
    z_keep,
    g_keep,
    u_keep,
    y_keep,
    e_stage,
    e_recv,
    p_keep,
    t_stage,
    t_recv,
    r_stage,
    r_recv,
    r_flat,
    o_wide,
    o_keep,
    arg_sem,
    local_sem,
    z_ssem,
    z_rsem,
    g_ssem,
    g_rsem,
    edge_ssem,
    edge_rsem,
    halo_ssem,
    halo_rsem,
    a_ssem,
    a_rsem,
    b_ssem,
    b_rsem,
    e_ssem,
    e_rsem,
    t_ssem,
    t_rsem,
    r_ssem,
    r_rsem,
    o_lsem,
    o_ssem,
    o_rsem,
):
    modes = decay_hbm.shape[0]
    share = 16 // ns
    rows = feat_ref.shape[1]
    block = 2 * rows
    steps = rows // RUNS
    pairs = nz // 2
    chan = lax.axis_index("chan")
    seq = lax.axis_index("seq")
    z = chan // 2
    k = chan % 2
    other = 1 - k
    position = seq * nz + z
    first = position == 0
    last = position == nz * ns - 1
    f32 = jnp.float32

    def dev(zz, kk, ss):
        return {"chan": zz * 2 + kk, "seq": ss}

    def remote(src, dst, ssem, rsem, device):
        return pltpu.make_async_remote_copy(
            src_ref=src, dst_ref=dst, send_sem=ssem, recv_sem=rsem, device_id=device, device_id_type=MESH
        )

    def local(src, dst, sem):
        return pltpu.make_async_copy(src, dst, sem)

    def wait_bytes(ref, sem):
        pltpu.make_async_copy(ref, ref, sem).wait()

    def far_first(n, of=nz):
        return (of // 2 + ((n + 1) // 2) * (1 - 2 * (n % 2))) % of

    def cols(j, kk):
        return pl.ds(pl.multiple_of((2 * j + kk) * LANES, LANES), LANES)

    my_rows = pl.ds(pl.multiple_of(k * rows, rows), rows)
    other_rows = pl.ds(pl.multiple_of(other * rows, rows), rows)

    barrier = pltpu.get_barrier_semaphore()

    def hello(device):
        pl.semaphore_signal(barrier, inc=1, device_id=device, device_id_type=MESH)

    for n in range(nz - 1):
        hello(dev((z + far_first(n)) % nz, k, seq))
    for n in range(1, ns):
        hello(dev(z, k, (seq + n) % ns))
    hello(dev(z, other, seq))
    before = position - 1 + nz * ns
    after = position + 1

    @pl.when(jnp.logical_not(first))
    def _():
        hello(dev(before % nz, 1, (before // nz) % ns))

    sends_halo = jnp.logical_and(k == 1, jnp.logical_not(last))

    wide_cols = 4 * LANES

    def chunk(p):
        at = pl.ds(pl.multiple_of(p * wide_cols, wide_cols), wide_cols)
        return local(feat_ref.at[:, :, at], feats.at[p], local_sem.at[p])

    def fetch(p, c):
        chunk(p).start()
        return c

    left, right = slice(0, block), slice(block, 2 * block)
    smalls = [
        (taps_hbm, taps_ref.at[pl.ds(0, 3)]),
        (decay_hbm, decay_ref),
        (res_hbm, res_ref),
        (skip_hbm, skip_ref),
        (mom_hbm.at[0], mom_ref.at[:, left]),
        (mom_hbm.at[1], mom_ref.at[:, right]),
        (toep_hbm.at[0], toep_ref.at[:, left]),
        (toep_hbm.at[1], toep_ref.at[:, right]),
        (cross_hbm, cross_ref),
    ]

    def ready(numbers):
        for i in numbers:
            local(*smalls[i], arg_sem.at[i]).wait()

    local(*smalls[0], arg_sem.at[0]).start()
    lax.fori_loop(0, pairs, fetch, 0)
    for i, (src, dst) in enumerate(smalls[1:]):
        local(src, dst, arg_sem.at[1 + i]).start()
    ready((0,))

    row_id = lax.broadcasted_iota(jnp.int32, (RUNS, LANES), 0)

    def spread(row):
        return jnp.broadcast_to(row, (RUNS, LANES))

    def run_rows(i, base=0):
        return pl.ds(base + i, RUNS, stride=steps)

    def conv(p, c):
        chunk(p).wait()
        for h in range(2):
            j = 2 * p + h
            for mine in (True, False):
                kk = k if mine else other
                at = pl.ds(pl.multiple_of((2 * h + kk) * LANES, LANES), LANES)
                streams = []
                for q in range(3):
                    wide[q] = feats[p, q, :, at].astype(f32)
                    tap = [spread(taps_ref[q, t : t + 1, cols(j, kk)]) for t in range(3)]
                    own = [wide[q, run_rows(i), :] for i in range(steps)]
                    seen = [pltpu.roll(own[-2], 1, axis=0), pltpu.roll(own[-1], 1, axis=0)] + own
                    streams.append(
                        [tap[0] * seen[i + 2] + tap[1] * seen[i + 1] + tap[2] * seen[i] for i in range(steps)]
                    )
                    ends = [wide[q, 0:2, :], wide[q, rows - 2 : rows, :]]
                    kept = edges.at[k] if mine else edge_out
                    kept[j, q, 0:2, :] = ends[0]
                    kept[j, q, 2:4, :] = ends[1]
                    halo_wide[kk, pl.ds(j * 6 + 2 * q, 2), :] = ends[1]
                gate = jnp.concatenate(streams[0], axis=0).astype(jnp.bfloat16)
                product = jnp.concatenate([streams[1][i] * streams[2][i] for i in range(steps)], axis=0)
                product = product.astype(jnp.bfloat16)
                lanes = pl.ds(h * LANES, LANES)
                if mine:
                    z_keep[p, my_rows, lanes] = product
                    g_keep[j, my_rows, :] = gate
                else:
                    z_out[p, :, lanes] = product
                    g_out[j] = gate
        return c

    lax.fori_loop(0, pairs, conv, 0)
    halo_send[...] = halo_wide[:, 0 : 6 * nz, :].astype(jnp.bfloat16)

    ready((1, 2, 3))
    decay = decay_ref[...]
    weight = res_ref[...] * jnp.sqrt(one_minus_exp_neg(2.0 * decay))
    half_a = decay * (block / 4.0)
    square = half_a * half_a
    lead = jnp.exp(-2.0 * half_a)
    for t in range(TERMS):
        total = jnp.ones_like(square)
        for i in range(10, 0, -1):
            total = 1.0 + square * (1.0 / (i * (i + t))) * total
        coef = lead * total * (1.0 if t == 0 else 2.0)
        lead = lead * half_a * (-1.0 / (t + 1))
        c_keep[0, t] = coef
        c_keep[1, t] = weight * coef
        h_src[t] = jnp.sum(weight * coef, axis=0, keepdims=True)
    for t in range(TERMS, 16):
        h_src[t] = skip_ref[...]
    r_flat[...] = jnp.zeros_like(r_flat)

    pl.semaphore_wait(barrier, (nz - 1) + (ns - 1) + 1 + 2 * sends_halo.astype(jnp.int32))

    @pl.when(sends_halo)
    def _():
        for kk in range(2):
            remote(
                halo_send.at[kk], halo_recv, halo_ssem, halo_rsem, dev(after % nz, kk, (after // nz) % ns)
            ).start()

    edge_copy = remote(edge_out.at[pl.ds(0, nz)], edges.at[k], edge_ssem, edge_rsem, dev(z, other, seq))
    edge_copy.start()

    def z_copy(p):
        return remote(z_out.at[p], z_keep.at[p, my_rows, :], z_ssem, z_rsem.at[p], dev(z, other, seq))

    def swap(n, c):
        z_copy((z // 2 + far_first(n, pairs)) % pairs).start()
        return c

    lax.fori_loop(0, pairs, swap, 0)

    my_rows_h = h_src.at[pl.ds(seq * share, share)]

    def send_a(n, c):
        remote(my_rows_h, h_col.at[z], a_ssem, a_rsem, dev((z + far_first(n)) % nz, k, seq)).start()
        return c

    lax.fori_loop(0, nz - 1, send_a, 0)
    local(my_rows_h, h_col.at[z], a_rsem).start()

    remote(g_out, g_keep.at[:, my_rows, :], g_ssem, g_rsem, dev(z, other, seq)).start()

    @pl.when(first)
    def _():
        halo_past[...] = jnp.zeros_like(halo_past)

    @pl.when(jnp.logical_not(first))
    def _():
        wait_bytes(halo_recv, halo_rsem)
        halo_past[0 : 6 * nz, :] = halo_recv[...].astype(f32)

    ready((4, 5))
    wait_bytes(edge_out.at[pl.ds(0, nz)], edge_rsem)

    def two_first(q, j, h):
        now = edges[h, j, q, 0:2, :]
        past = halo_past[pl.ds(j * 6 + 2 * q, 2), :] if h == 0 else edges[0, j, q, 2:4, :]
        tap = [taps_ref[q, t : t + 1, cols(j, k)] for t in range(3)]
        one = tap[0] * now[0:1] + tap[1] * past[1:2] + tap[2] * past[0:1]
        two = tap[0] * now[1:2] + tap[1] * now[0:1] + tap[2] * past[1:2]
        return one, two

    tile_row = lax.broadcasted_iota(jnp.int32, (16, LANES), 0)

    def mend(old, one, two):
        fresh = jnp.where(tile_row == 0, jnp.broadcast_to(one, (16, LANES)), old.astype(f32))
        fresh = jnp.where(tile_row == RUNS, jnp.broadcast_to(two, (16, LANES)), fresh)
        return fresh.astype(jnp.bfloat16)

    def forward(n, c):
        p = (z // 2 + far_first(n, pairs)) % pairs
        wait_bytes(z_out.at[p], z_rsem.at[p])
        for h in range(2):
            lanes = pl.ds(h * LANES, LANES)
            for core in range(2):
                at = pl.ds(core * rows, 16)
                second, third = two_first(1, 2 * p + h, core), two_first(2, 2 * p + h, core)
                z_keep[p, at, lanes] = mend(z_keep[p, at, lanes], second[0] * third[0], second[1] * third[1])
        kept = z_keep[p]
        found = jnp.dot(mom_ref[...], jnp.concatenate([kept, kept], axis=0), preferred_element_type=f32)
        found = found[0:16] + found[16:32]
        for h in range(2):
            j = 2 * p + h
            e_stage[j] = found[:, h * LANES : (h + 1) * LANES].astype(jnp.bfloat16)

            @pl.when(j != z)
            def _():
                remote(e_stage.at[j], e_recv.at[z], e_ssem, e_rsem, dev(j, k, seq)).start()

            @pl.when(j == z)
            def _():
                local(e_stage.at[j], e_recv.at[z], e_rsem).start()

        return c

    lax.fori_loop(0, pairs, forward, 0)

    def inner(p, c):
        kept = z_keep[p]
        u_keep[...] = jnp.dot(
            toep_ref[...], jnp.concatenate([kept, kept], axis=0), preferred_element_type=f32
        )
        for h in range(2):
            j = 2 * p + h
            lanes = slice(h * LANES, (h + 1) * LANES)
            hs = [spread(h_all[t // share, j, t % share]) for t in range(TERMS)]
            skip = spread(h_all[TERMS // share, j, TERMS % share])
            for i in range(0, 2 * steps, 2):
                kept = z_keep[p, i * RUNS : (i + 2) * RUNS, lanes].astype(f32)
                for b in range(2):
                    row = (i + b) * RUNS
                    total = skip * kept[b * RUNS : (b + 1) * RUNS]
                    for t in range(TERMS):
                        total = total + hs[t] * u_keep[t * block + row : t * block + row + RUNS, lanes]
                    y_keep[j, row : row + RUNS, :] = total
        return c

    wait_bytes(h_col, a_rsem)

    def send_b(n, c):
        remote(h_col, h_all.at[seq], b_ssem, b_rsem, dev(z, k, (seq + n) % ns)).start()
        return c

    lax.fori_loop(1, ns, send_b, 0)
    local(h_col, h_all.at[seq], b_rsem).start()

    wait_bytes(e_recv, e_rsem)
    block_decay = jnp.exp(-decay * float(block))

    def along_z(zz, state):
        p_keep[zz] = state
        got = e_recv[zz].astype(f32)
        added = c_keep[0, 0] * got[0:1]
        for t in range(1, TERMS):
            added = added + c_keep[0, t] * got[t : t + 1]
        return block_decay * state + added

    t_stage[...] = lax.fori_loop(0, nz, along_z, jnp.zeros_like(decay)).astype(jnp.bfloat16)

    def send_t(ss, c):
        remote(t_stage, t_recv.at[seq], t_ssem.at[ss], t_rsem.at[seq], dev(z, k, ss)).start()
        return c

    lax.fori_loop(seq + 1, ns, send_t, 0)

    seq_decay = jnp.exp(-decay * float(block * nz))

    def along_s(ss, state):
        wait_bytes(t_recv.at[ss], t_rsem.at[ss])
        return seq_decay * state + t_recv[ss].astype(f32)

    incoming = lax.fori_loop(0, seq, along_s, jnp.zeros_like(decay))

    def send_r(n, c):
        zz = (z + far_first(n)) % nz
        state = p_keep[zz] + jnp.exp(-decay * (zz * block).astype(f32)) * incoming
        for t in range(TERMS):
            r_flat[t : t + 1, :] = jnp.sum(c_keep[1, t] * state, axis=0, keepdims=True)
        r_stage[zz] = r_flat[...].astype(jnp.bfloat16)

        @pl.when(n < nz - 1)
        def _():
            remote(r_stage.at[zz], r_recv.at[z], r_ssem, r_rsem.at[z], dev(zz, k, seq)).start()

        @pl.when(n == nz - 1)
        def _():
            local(r_stage.at[zz], r_recv.at[z], r_rsem.at[z]).start()

        return c

    lax.fori_loop(0, nz, send_r, 0)
    wait_bytes(h_all, b_rsem)
    ready((6, 7, 8))
    lax.fori_loop(0, pairs, inner, 0)

    def finish(n, c):
        p = (z // 2 + far_first(pairs - 1 - n, pairs)) % (pairs)
        for h in range(2):
            j = 2 * p + h
            wait_bytes(r_recv.at[j], r_rsem.at[j])
        coef = jnp.concatenate([r_recv[2 * p], r_recv[2 * p + 1]], axis=1)
        none = jnp.zeros_like(coef)
        stacked = jnp.concatenate([coef, coef] + [none] * 6, axis=0)
        reached = jnp.dot(cross_ref[...], stacked, preferred_element_type=f32)
        for h in range(2):
            j = 2 * p + h
            for core in range(2):
                at = pl.ds(core * rows, 16)
                one, two = two_first(0, j, core)
                g_keep[j, at, :] = mend(g_keep[j, at, :], one, two)
            for i in range(0, 2 * steps, 2):
                gate = g_keep[j, i * RUNS : (i + 2) * RUNS, :].astype(f32)
                for b in range(2):
                    at = slice((i + b) * RUNS, (i + b + 1) * RUNS)
                    half, step = (i + b) // steps, (i + b) % steps
                    o_wide[h, run_rows(step, half * rows), :] = gate[b * RUNS : (b + 1) * RUNS] * (
                        y_keep[j, at, :] + reached[at, h * LANES : (h + 1) * LANES]
                    )
            o_keep[j] = o_wide[h].astype(jnp.bfloat16)
            local(o_keep.at[j, my_rows, :], out_ref.at[:, cols(j, k)], o_lsem).start()
            remote(
                o_keep.at[j, other_rows, :], out_ref.at[:, cols(j, k)], o_ssem, o_rsem, dev(z, other, seq)
            ).start()
        return c

    wait_bytes(g_out, g_rsem)
    lax.fori_loop(0, pairs, finish, 0)

    half = out_ref.at[:, pl.ds(0, nz * LANES)]
    wait_bytes(half, o_lsem)
    wait_bytes(half, o_ssem)
    wait_bytes(half, o_rsem)
    wait_bytes(z_out, z_ssem)
    wait_bytes(g_out, g_ssem)
    wait_bytes(edge_out.at[pl.ds(0, nz)], edge_ssem)
    wait_bytes(h_col.at[pl.ds(0, nz - 1)], a_ssem)
    wait_bytes(h_all.at[pl.ds(0, ns - 1)], b_ssem)
    wait_bytes(e_recv.at[pl.ds(0, nz - 1)], e_ssem)

    def sent_t(ss, c):
        wait_bytes(t_stage, t_ssem.at[ss])
        return c

    lax.fori_loop(seq + 1, ns, sent_t, 0)
    wait_bytes(r_recv.at[pl.ds(0, nz - 1)], r_ssem)

    @pl.when(sends_halo)
    def _():
        wait_bytes(halo_send, halo_ssem)


def per_device(nz, ns, features, short_taps, decay_rates, residues, skip_gain):
    streams, rows, width = features.shape
    modes = decay_rates.shape[0]
    block = 2 * rows
    pairs = nz // 2
    toeplitz, moments, cross = fixed_matrices(block)
    f32 = jnp.float32
    bf16 = jnp.bfloat16
    hbm = pl.BlockSpec(memory_space=pltpu.HBM)
    anywhere = pl.BlockSpec(memory_space=pl.ANY)
    dma = pltpu.SemaphoreType.DMA
    return pl.pallas_call(
        functools.partial(kernel, nz, ns),
        out_shape=jax.ShapeDtypeStruct((rows, width), jnp.bfloat16),
        in_specs=[hbm] * 8,
        out_specs=anywhere,
        scratch_shapes=[
            pltpu.VMEM((4,) + short_taps.shape[1:], f32),
            pltpu.VMEM((modes, LANES), f32),
            pltpu.VMEM((modes, LANES), f32),
            pltpu.VMEM((1, LANES), f32),
            pltpu.VMEM((TERMS * block, 2 * block), bf16),
            pltpu.VMEM((32, 2 * block), bf16),
            pltpu.VMEM(cross.shape, bf16),
            pltpu.VMEM((pairs, streams, rows, 4 * LANES), bf16),
            pltpu.VMEM((2, nz * 2 * streams + 16, LANES), f32),
            pltpu.VMEM((2, nz * 2 * streams, LANES), bf16),
            pltpu.VMEM((nz * 2 * streams, LANES), bf16),
            pltpu.VMEM((nz * 2 * streams + 16, LANES), f32),
            pltpu.VMEM((nz + 1, streams, 4, LANES), f32),
            pltpu.VMEM((3, nz, streams, 4, LANES), f32),
            pltpu.VMEM((pairs, rows, 2 * LANES), bf16),
            pltpu.VMEM((nz, rows, LANES), bf16),
            pltpu.VMEM((24, 1, LANES), f32),
            pltpu.VMEM((nz, 16 // ns, 1, LANES), f32),
            pltpu.VMEM((ns, nz, 16 // ns, 1, LANES), f32),
            pltpu.VMEM((2, TERMS, modes, LANES), f32),
            pltpu.VMEM((streams + 1, rows, LANES), f32),
            pltpu.VMEM((pairs, block, 2 * LANES), bf16),
            pltpu.VMEM((nz, block, LANES), bf16),
            pltpu.VMEM((TERMS * block, 2 * LANES), f32),
            pltpu.VMEM((nz, block, LANES), f32),
            pltpu.VMEM((nz, 16, LANES), bf16),
            pltpu.VMEM((nz, 16, LANES), bf16),
            pltpu.VMEM((nz, modes, LANES), f32),
            pltpu.VMEM((modes, LANES), bf16),
            pltpu.VMEM((ns, modes, LANES), bf16),
            pltpu.VMEM((nz, 16, LANES), bf16),
            pltpu.VMEM((nz, 16, LANES), bf16),
            pltpu.VMEM((16, LANES), f32),
            pltpu.VMEM((3, block, LANES), f32),
            pltpu.VMEM((nz, block, LANES), bf16),
            dma((9,)),
            dma((pairs,)),
            dma,
            dma((pairs,)),
            dma,
            dma,
            dma,
            dma,
            dma,
            dma,
            dma,
            dma,
            dma,
            dma,
            dma,
            dma,
            dma((ns,)),
            dma((ns,)),
            dma,
            dma((nz,)),
            dma,
            dma,
            dma,
        ],
        compiler_params=pltpu.CompilerParams(
            collective_id=0, has_side_effects=True, vmem_limit_bytes=60 * 1024 * 1024
        ),
        cost_estimate=pl.CostEstimate(flops=40_000_000, bytes_accessed=2_200_000, transcendentals=0),
    )(short_taps, decay_rates, residues, skip_gain.reshape(1, -1), toeplitz, moments, cross, features)


def solution(mesh):
    nz, ns = mesh.shape["chan"] // 2, mesh.shape["seq"]
    placed = (P(None, ("seq", "chan"), None), P(), P(None, "chan"), P(None, "chan"), P("chan"))
    return jax.shard_map(
        functools.partial(per_device, nz, ns),
        mesh=mesh,
        in_specs=placed,
        out_specs=P(("seq", "chan"), None),
        check_vma=False,
    )
```

```python
import functools

import jax
import jax.numpy as jnp
import ml_dtypes
import numpy as np
from jax import lax
from jax.experimental import pallas as pl
from jax.experimental.pallas import tpu as pltpu
from jax.sharding import PartitionSpec as P

MESH = pl.DeviceIdType.MESH
LANES = 128
RUNS = 8
TERMS = 12


def fixed_matrices(block):
    half = block // 2
    steps = half // RUNS
    rows = np.arange(half)
    token = steps * (rows % RUNS) + rows // RUNS
    token = np.concatenate([token, half + token])

    def polys(lag):
        u = 2.0 * lag / block - 1.0
        out = [np.ones_like(u), u]
        while len(out) < TERMS:
            out.append(2.0 * u * out[-1] - out[-2])
        return np.stack(out)

    def parts(x):
        found = []
        for _ in range(3):
            found.append(x.astype(ml_dtypes.bfloat16))
            x = x - found[-1].astype(np.float64)
        return found

    lag = token[:, None] - token[None, :]
    inside = np.where(lag >= 0, polys(np.maximum(lag, 0).astype(np.float64)), 0.0)
    first, second, _ = parts(inside.reshape(TERMS * block, block))
    toeplitz = np.stack([first, second])

    end = np.zeros((16, block))
    end[:TERMS] = polys((block - 1 - token).astype(np.float64))
    first, second, third = parts(end)
    moments = np.stack([np.concatenate([first, third]), np.concatenate([second, 0 * third])])

    reach = np.zeros((block, 16))
    reach[:, :TERMS] = polys((token + 1).astype(np.float64)).T
    first, second, _ = parts(reach)
    none = 0 * first
    cross = np.concatenate([first, second] + [none] * 6, axis=1)
    return toeplitz, moments, cross


def one_minus_exp_neg(u):
    series = 1.0 - u * (1.0 / 8.0)
    for n in (7, 6, 5, 4, 3, 2):
        series = 1.0 - (u * (1.0 / n)) * series
    return jnp.where(u < 0.25, u * series, 1.0 - jnp.exp(-u))


def kernel(
    nz,
    ns,
    taps_hbm,
    decay_hbm,
    res_hbm,
    skip_hbm,
    toep_hbm,
    mom_hbm,
    cross_hbm,
    feat_ref,
    out_ref,
    taps_ref,
    decay_ref,
    res_ref,
    skip_ref,
    toep_ref,
    mom_ref,
    cross_ref,
    feats,
    halo_wide,
    halo_send,
    halo_recv,
    halo_past,
    edge_out,
    edges,
    z_out,
    g_out,
    h_src,
    h_col,
    h_all,
    c_keep,
    wide,
    z_keep,
    g_keep,
    u_keep,
    y_keep,
    e_stage,
    e_recv,
    a_keep,
    p_keep,
    t_stage,
    t_recv,
    r_stage,
    r_recv,
    r_flat,
    o_wide,
    o_keep,
    arg_sem,
    local_sem,
    z_ssem,
    z_rsem,
    g_ssem,
    g_rsem,
    edge_ssem,
    edge_rsem,
    halo_ssem,
    halo_rsem,
    a_ssem,
    a_rsem,
    b_ssem,
    b_rsem,
    e_ssem,
    e_rsem,
    t_ssem,
    t_rsem,
    r_ssem,
    r_rsem,
    o_lsem,
    o_ssem,
    o_rsem,
):
    modes = decay_hbm.shape[0]
    share = 16 // ns
    rows = feat_ref.shape[1]
    block = 2 * rows
    steps = rows // RUNS
    pairs = nz // 2
    chan = lax.axis_index("chan")
    seq = lax.axis_index("seq")
    z = chan // 2
    k = chan % 2
    other = 1 - k
    position = seq * nz + z
    first = position == 0
    last = position == nz * ns - 1
    f32 = jnp.float32

    def dev(zz, kk, ss):
        return {"chan": zz * 2 + kk, "seq": ss}

    def remote(src, dst, ssem, rsem, device):
        return pltpu.make_async_remote_copy(
            src_ref=src, dst_ref=dst, send_sem=ssem, recv_sem=rsem, device_id=device, device_id_type=MESH
        )

    def local(src, dst, sem):
        return pltpu.make_async_copy(src, dst, sem)

    def wait_bytes(ref, sem):
        pltpu.make_async_copy(ref, ref, sem).wait()

    def far_first(n, of=nz):
        return (of // 2 + ((n + 1) // 2) * (1 - 2 * (n % 2))) % of

    def cols(j, kk):
        return pl.ds(pl.multiple_of((2 * j + kk) * LANES, LANES), LANES)

    my_rows = pl.ds(pl.multiple_of(k * rows, rows), rows)
    other_rows = pl.ds(pl.multiple_of(other * rows, rows), rows)

    barrier = pltpu.get_barrier_semaphore()

    def hello(device):
        pl.semaphore_signal(barrier, inc=1, device_id=device, device_id_type=MESH)

    for n in range(nz - 1):
        hello(dev((z + far_first(n)) % nz, k, seq))
    for n in range(1, ns):
        hello(dev(z, k, (seq + n) % ns))
    hello(dev(z, other, seq))
    before = position - 1 + nz * ns
    after = position + 1

    @pl.when(jnp.logical_not(first))
    def _():
        hello(dev(before % nz, 1, (before // nz) % ns))

    sends_halo = jnp.logical_and(k == 1, jnp.logical_not(last))

    wide_cols = 4 * LANES

    def chunk(p):
        at = pl.ds(pl.multiple_of(p * wide_cols, wide_cols), wide_cols)
        return local(feat_ref.at[:, :, at], feats.at[p], local_sem.at[p])

    def fetch(p, c):
        chunk(p).start()
        return c

    left, right = slice(0, block), slice(block, 2 * block)
    smalls = [
        (taps_hbm, taps_ref.at[pl.ds(0, 3)]),
        (decay_hbm, decay_ref),
        (res_hbm, res_ref),
        (skip_hbm, skip_ref),
        (mom_hbm.at[0], mom_ref.at[:, left]),
        (mom_hbm.at[1], mom_ref.at[:, right]),
        (toep_hbm.at[0], toep_ref.at[:, left]),
        (toep_hbm.at[1], toep_ref.at[:, right]),
        (cross_hbm, cross_ref),
    ]

    def ready(numbers):
        for i in numbers:
            local(*smalls[i], arg_sem.at[i]).wait()

    local(*smalls[0], arg_sem.at[0]).start()
    lax.fori_loop(0, pairs, fetch, 0)
    for i, (src, dst) in enumerate(smalls[1:]):
        local(src, dst, arg_sem.at[1 + i]).start()
    ready((0,))

    row_id = lax.broadcasted_iota(jnp.int32, (RUNS, LANES), 0)

    def spread(row):
        return jnp.broadcast_to(row, (RUNS, LANES))

    def run_rows(i, base=0):
        return pl.ds(base + i, RUNS, stride=steps)

    def conv(p, c):
        chunk(p).wait()
        for h in range(2):
            j = 2 * p + h
            for mine in (True, False):
                kk = k if mine else other
                at = pl.ds(pl.multiple_of((2 * h + kk) * LANES, LANES), LANES)
                streams = []
                for q in range(3):
                    wide[q] = feats[p, q, :, at].astype(f32)
                    tap = [spread(taps_ref[q, t : t + 1, cols(j, kk)]) for t in range(3)]
                    own = [wide[q, run_rows(i), :] for i in range(steps)]
                    seen = [pltpu.roll(own[-2], 1, axis=0), pltpu.roll(own[-1], 1, axis=0)] + own
                    streams.append(
                        [tap[0] * seen[i + 2] + tap[1] * seen[i + 1] + tap[2] * seen[i] for i in range(steps)]
                    )
                    ends = [wide[q, 0:2, :], wide[q, rows - 2 : rows, :]]
                    kept = edges.at[k] if mine else edge_out
                    kept[j, q, 0:2, :] = ends[0]
                    kept[j, q, 2:4, :] = ends[1]
                    halo_wide[kk, pl.ds(j * 6 + 2 * q, 2), :] = ends[1]
                gate = jnp.concatenate(streams[0], axis=0).astype(jnp.bfloat16)
                product = jnp.concatenate([streams[1][i] * streams[2][i] for i in range(steps)], axis=0)
                product = product.astype(jnp.bfloat16)
                lanes = pl.ds(h * LANES, LANES)
                if mine:
                    z_keep[p, my_rows, lanes] = product
                    g_keep[j, my_rows, :] = gate
                else:
                    z_out[p, :, lanes] = product
                    g_out[j] = gate
        return c

    lax.fori_loop(0, pairs, conv, 0)
    halo_send[...] = halo_wide[:, 0 : 6 * nz, :].astype(jnp.bfloat16)

    ready((1, 2, 3))
    decay = decay_ref[...]
    weight = res_ref[...] * jnp.sqrt(one_minus_exp_neg(2.0 * decay))
    half_a = decay * (block / 4.0)
    square = half_a * half_a
    lead = jnp.exp(-2.0 * half_a)
    for t in range(TERMS):
        total = jnp.ones_like(square)
        for i in range(10, 0, -1):
            total = 1.0 + square * (1.0 / (i * (i + t))) * total
        coef = lead * total * (1.0 if t == 0 else 2.0)
        lead = lead * half_a * (-1.0 / (t + 1))
        c_keep[0, t] = coef
        c_keep[1, t] = weight * coef
        h_src[t] = jnp.sum(weight * coef, axis=0, keepdims=True)
    for t in range(TERMS, 16):
        h_src[t] = skip_ref[...]
    r_flat[...] = jnp.zeros_like(r_flat)

    pl.semaphore_wait(barrier, (nz - 1) + (ns - 1) + 1 + 2 * sends_halo.astype(jnp.int32))

    @pl.when(sends_halo)
    def _():
        for kk in range(2):
            remote(
                halo_send.at[kk], halo_recv, halo_ssem, halo_rsem, dev(after % nz, kk, (after // nz) % ns)
            ).start()

    edge_copy = remote(edge_out.at[pl.ds(0, nz)], edges.at[k], edge_ssem, edge_rsem, dev(z, other, seq))
    edge_copy.start()

    def z_copy(p):
        return remote(z_out.at[p], z_keep.at[p, my_rows, :], z_ssem, z_rsem.at[p], dev(z, other, seq))

    def swap(n, c):
        z_copy((z // 2 + far_first(n, pairs)) % pairs).start()
        return c

    lax.fori_loop(0, pairs, swap, 0)

    my_rows_h = h_src.at[pl.ds(seq * share, share)]

    def send_a(n, c):
        remote(my_rows_h, h_col.at[z], a_ssem, a_rsem, dev((z + far_first(n)) % nz, k, seq)).start()
        return c

    lax.fori_loop(0, nz - 1, send_a, 0)
    local(my_rows_h, h_col.at[z], a_rsem).start()

    remote(g_out, g_keep.at[:, my_rows, :], g_ssem, g_rsem, dev(z, other, seq)).start()

    @pl.when(first)
    def _():
        halo_past[...] = jnp.zeros_like(halo_past)

    @pl.when(jnp.logical_not(first))
    def _():
        wait_bytes(halo_recv, halo_rsem)
        halo_past[0 : 6 * nz, :] = halo_recv[...].astype(f32)

    ready((4, 5))
    wait_bytes(edge_out.at[pl.ds(0, nz)], edge_rsem)

    def two_first(q, j, h):
        now = edges[h, j, q, 0:2, :]
        past = halo_past[pl.ds(j * 6 + 2 * q, 2), :] if h == 0 else edges[0, j, q, 2:4, :]
        tap = [taps_ref[q, t : t + 1, cols(j, k)] for t in range(3)]
        one = tap[0] * now[0:1] + tap[1] * past[1:2] + tap[2] * past[0:1]
        two = tap[0] * now[1:2] + tap[1] * now[0:1] + tap[2] * past[1:2]
        return one, two

    tile_row = lax.broadcasted_iota(jnp.int32, (16, LANES), 0)

    def mend(old, one, two):
        fresh = jnp.where(tile_row == 0, jnp.broadcast_to(one, (16, LANES)), old.astype(f32))
        fresh = jnp.where(tile_row == RUNS, jnp.broadcast_to(two, (16, LANES)), fresh)
        return fresh.astype(jnp.bfloat16)

    def forward(n, c):
        p = (z // 2 + far_first(n, pairs)) % pairs
        wait_bytes(z_out.at[p], z_rsem.at[p])
        for h in range(2):
            lanes = pl.ds(h * LANES, LANES)
            for core in range(2):
                at = pl.ds(core * rows, 16)
                second, third = two_first(1, 2 * p + h, core), two_first(2, 2 * p + h, core)
                z_keep[p, at, lanes] = mend(z_keep[p, at, lanes], second[0] * third[0], second[1] * third[1])
        kept = z_keep[p]
        found = jnp.dot(mom_ref[...], jnp.concatenate([kept, kept], axis=0), preferred_element_type=f32)
        found = found[0:16] + found[16:32]
        for h in range(2):
            j = 2 * p + h
            e_stage[j] = found[:, h * LANES : (h + 1) * LANES].astype(jnp.bfloat16)

            @pl.when(j != z)
            def _():
                remote(e_stage.at[j], e_recv.at[z], e_ssem, e_rsem.at[z], dev(j, k, seq)).start()

            @pl.when(j == z)
            def _():
                local(e_stage.at[j], e_recv.at[z], e_rsem.at[z]).start()

        return c

    lax.fori_loop(0, pairs, forward, 0)

    def inner(p, c):
        kept = z_keep[p]
        u_keep[...] = jnp.dot(
            toep_ref[...], jnp.concatenate([kept, kept], axis=0), preferred_element_type=f32
        )
        for h in range(2):
            j = 2 * p + h
            lanes = slice(h * LANES, (h + 1) * LANES)
            hs = [spread(h_all[t // share, j, t % share]) for t in range(TERMS)]
            skip = spread(h_all[TERMS // share, j, TERMS % share])
            for i in range(0, 2 * steps, 2):
                kept = z_keep[p, i * RUNS : (i + 2) * RUNS, lanes].astype(f32)
                for b in range(2):
                    row = (i + b) * RUNS
                    total = skip * kept[b * RUNS : (b + 1) * RUNS]
                    for t in range(TERMS):
                        total = total + hs[t] * u_keep[t * block + row : t * block + row + RUNS, lanes]
                    y_keep[j, row : row + RUNS, :] = total
        return c

    wait_bytes(h_col, a_rsem)

    def send_b(n, c):
        remote(h_col, h_all.at[seq], b_ssem, b_rsem, dev(z, k, (seq + n) % ns)).start()
        return c

    lax.fori_loop(1, ns, send_b, 0)
    local(h_col, h_all.at[seq], b_rsem).start()

    block_decay = jnp.exp(-decay * float(block))

    def take(n, c):
        zz = (z + far_first(nz - 1 - n)) % nz
        wait_bytes(e_recv.at[zz], e_rsem.at[zz])
        got = e_recv[zz].astype(f32)
        added = c_keep[0, 0] * got[0:1]
        for t in range(1, TERMS):
            added = added + c_keep[0, t] * got[t : t + 1]
        a_keep[zz] = added
        return c

    lax.fori_loop(0, nz, take, 0)

    def along_z(zz, state):
        p_keep[zz] = state
        return block_decay * state + a_keep[zz]

    t_stage[...] = lax.fori_loop(0, nz, along_z, jnp.zeros_like(decay)).astype(jnp.bfloat16)

    def send_t(ss, c):
        remote(t_stage, t_recv.at[seq], t_ssem.at[ss], t_rsem.at[seq], dev(z, k, ss)).start()
        return c

    lax.fori_loop(seq + 1, ns, send_t, 0)

    seq_decay = jnp.exp(-decay * float(block * nz))

    def along_s(ss, state):
        wait_bytes(t_recv.at[ss], t_rsem.at[ss])
        return seq_decay * state + t_recv[ss].astype(f32)

    incoming = lax.fori_loop(0, seq, along_s, jnp.zeros_like(decay))

    def send_r(n, c):
        zz = (z + far_first(n)) % nz
        state = p_keep[zz] + jnp.exp(-decay * (zz * block).astype(f32)) * incoming
        for t in range(TERMS):
            r_flat[t : t + 1, :] = jnp.sum(c_keep[1, t] * state, axis=0, keepdims=True)
        r_stage[zz] = r_flat[...].astype(jnp.bfloat16)

        @pl.when(n < nz - 1)
        def _():
            remote(r_stage.at[zz], r_recv.at[z], r_ssem, r_rsem.at[z], dev(zz, k, seq)).start()

        @pl.when(n == nz - 1)
        def _():
            local(r_stage.at[zz], r_recv.at[z], r_rsem.at[z]).start()

        return c

    lax.fori_loop(0, nz, send_r, 0)
    wait_bytes(h_all, b_rsem)
    ready((6, 7, 8))
    lax.fori_loop(0, pairs, inner, 0)

    def finish(n, c):
        p = (z // 2 + far_first(pairs - 1 - n, pairs)) % (pairs)
        for h in range(2):
            j = 2 * p + h
            wait_bytes(r_recv.at[j], r_rsem.at[j])
        coef = jnp.concatenate([r_recv[2 * p], r_recv[2 * p + 1]], axis=1)
        none = jnp.zeros_like(coef)
        stacked = jnp.concatenate([coef, coef] + [none] * 6, axis=0)
        reached = jnp.dot(cross_ref[...], stacked, preferred_element_type=f32)
        for h in range(2):
            j = 2 * p + h
            for core in range(2):
                at = pl.ds(core * rows, 16)
                one, two = two_first(0, j, core)
                g_keep[j, at, :] = mend(g_keep[j, at, :], one, two)
            for i in range(0, 2 * steps, 2):
                gate = g_keep[j, i * RUNS : (i + 2) * RUNS, :].astype(f32)
                for b in range(2):
                    at = slice((i + b) * RUNS, (i + b + 1) * RUNS)
                    half, step = (i + b) // steps, (i + b) % steps
                    o_wide[h, run_rows(step, half * rows), :] = gate[b * RUNS : (b + 1) * RUNS] * (
                        y_keep[j, at, :] + reached[at, h * LANES : (h + 1) * LANES]
                    )
            o_keep[j] = o_wide[h].astype(jnp.bfloat16)
            local(o_keep.at[j, my_rows, :], out_ref.at[:, cols(j, k)], o_lsem).start()
            remote(
                o_keep.at[j, other_rows, :], out_ref.at[:, cols(j, k)], o_ssem, o_rsem, dev(z, other, seq)
            ).start()
        return c

    wait_bytes(g_out, g_rsem)
    lax.fori_loop(0, pairs, finish, 0)

    half = out_ref.at[:, pl.ds(0, nz * LANES)]
    wait_bytes(half, o_lsem)
    wait_bytes(half, o_ssem)
    wait_bytes(half, o_rsem)
    wait_bytes(z_out, z_ssem)
    wait_bytes(g_out, g_ssem)
    wait_bytes(edge_out.at[pl.ds(0, nz)], edge_ssem)
    wait_bytes(h_col.at[pl.ds(0, nz - 1)], a_ssem)
    wait_bytes(h_all.at[pl.ds(0, ns - 1)], b_ssem)
    wait_bytes(e_recv.at[pl.ds(0, nz - 1)], e_ssem)

    def sent_t(ss, c):
        wait_bytes(t_stage, t_ssem.at[ss])
        return c

    lax.fori_loop(seq + 1, ns, sent_t, 0)
    wait_bytes(r_recv.at[pl.ds(0, nz - 1)], r_ssem)

    @pl.when(sends_halo)
    def _():
        wait_bytes(halo_send, halo_ssem)


def per_device(nz, ns, features, short_taps, decay_rates, residues, skip_gain):
    streams, rows, width = features.shape
    modes = decay_rates.shape[0]
    block = 2 * rows
    pairs = nz // 2
    toeplitz, moments, cross = fixed_matrices(block)
    f32 = jnp.float32
    bf16 = jnp.bfloat16
    hbm = pl.BlockSpec(memory_space=pltpu.HBM)
    anywhere = pl.BlockSpec(memory_space=pl.ANY)
    dma = pltpu.SemaphoreType.DMA
    return pl.pallas_call(
        functools.partial(kernel, nz, ns),
        out_shape=jax.ShapeDtypeStruct((rows, width), jnp.bfloat16),
        in_specs=[hbm] * 8,
        out_specs=anywhere,
        scratch_shapes=[
            pltpu.VMEM((4,) + short_taps.shape[1:], f32),
            pltpu.VMEM((modes, LANES), f32),
            pltpu.VMEM((modes, LANES), f32),
            pltpu.VMEM((1, LANES), f32),
            pltpu.VMEM((TERMS * block, 2 * block), bf16),
            pltpu.VMEM((32, 2 * block), bf16),
            pltpu.VMEM(cross.shape, bf16),
            pltpu.VMEM((pairs, streams, rows, 4 * LANES), bf16),
            pltpu.VMEM((2, nz * 2 * streams + 16, LANES), f32),
            pltpu.VMEM((2, nz * 2 * streams, LANES), bf16),
            pltpu.VMEM((nz * 2 * streams, LANES), bf16),
            pltpu.VMEM((nz * 2 * streams + 16, LANES), f32),
            pltpu.VMEM((nz + 1, streams, 4, LANES), f32),
            pltpu.VMEM((3, nz, streams, 4, LANES), f32),
            pltpu.VMEM((pairs, rows, 2 * LANES), bf16),
            pltpu.VMEM((nz, rows, LANES), bf16),
            pltpu.VMEM((24, 1, LANES), f32),
            pltpu.VMEM((nz, 16 // ns, 1, LANES), f32),
            pltpu.VMEM((ns, nz, 16 // ns, 1, LANES), f32),
            pltpu.VMEM((2, TERMS, modes, LANES), f32),
            pltpu.VMEM((streams + 1, rows, LANES), f32),
            pltpu.VMEM((pairs, block, 2 * LANES), bf16),
            pltpu.VMEM((nz, block, LANES), bf16),
            pltpu.VMEM((TERMS * block, 2 * LANES), f32),
            pltpu.VMEM((nz, block, LANES), f32),
            pltpu.VMEM((nz, 16, LANES), bf16),
            pltpu.VMEM((nz, 16, LANES), bf16),
            pltpu.VMEM((nz, modes, LANES), f32),
            pltpu.VMEM((nz, modes, LANES), f32),
            pltpu.VMEM((modes, LANES), bf16),
            pltpu.VMEM((ns, modes, LANES), bf16),
            pltpu.VMEM((nz, 16, LANES), bf16),
            pltpu.VMEM((nz, 16, LANES), bf16),
            pltpu.VMEM((16, LANES), f32),
            pltpu.VMEM((3, block, LANES), f32),
            pltpu.VMEM((nz, block, LANES), bf16),
            dma((9,)),
            dma((pairs,)),
            dma,
            dma((pairs,)),
            dma,
            dma,
            dma,
            dma,
            dma,
            dma,
            dma,
            dma,
            dma,
            dma,
            dma,
            dma((nz,)),
            dma((ns,)),
            dma((ns,)),
            dma,
            dma((nz,)),
            dma,
            dma,
            dma,
        ],
        compiler_params=pltpu.CompilerParams(
            collective_id=0, has_side_effects=True, vmem_limit_bytes=60 * 1024 * 1024
        ),
        cost_estimate=pl.CostEstimate(flops=40_000_000, bytes_accessed=2_200_000, transcendentals=0),
    )(short_taps, decay_rates, residues, skip_gain.reshape(1, -1), toeplitz, moments, cross, features)


def solution(mesh):
    nz, ns = mesh.shape["chan"] // 2, mesh.shape["seq"]
    placed = (P(None, ("seq", "chan"), None), P(), P(None, "chan"), P(None, "chan"), P("chan"))
    return jax.shard_map(
        functools.partial(per_device, nz, ns),
        mesh=mesh,
        in_specs=placed,
        out_specs=P(("seq", "chan"), None),
        check_vma=False,
    )
```

```python
import functools

import jax
import jax.numpy as jnp
import ml_dtypes
import numpy as np
from jax import lax
from jax.experimental import pallas as pl
from jax.experimental.pallas import tpu as pltpu
from jax.sharding import PartitionSpec as P

MESH = pl.DeviceIdType.MESH
LANES = 128
RUNS = 8
TERMS = 12


def fixed_matrices(block):
    half = block // 2
    steps = half // RUNS
    rows = np.arange(half)
    token = steps * (rows % RUNS) + rows // RUNS
    token = np.concatenate([token, half + token])

    def polys(lag):
        u = 2.0 * lag / block - 1.0
        out = [np.ones_like(u), u]
        while len(out) < TERMS:
            out.append(2.0 * u * out[-1] - out[-2])
        return np.stack(out)

    def parts(x):
        found = []
        for _ in range(3):
            found.append(x.astype(ml_dtypes.bfloat16))
            x = x - found[-1].astype(np.float64)
        return found

    lag = token[:, None] - token[None, :]
    inside = np.where(lag >= 0, polys(np.maximum(lag, 0).astype(np.float64)), 0.0)
    first, second, _ = parts(inside.reshape(TERMS * block, block))
    toeplitz = np.stack([first, second])

    end = np.zeros((16, block))
    end[:TERMS] = polys((block - 1 - token).astype(np.float64))
    first, second, third = parts(end)
    moments = np.stack([np.concatenate([first, third]), np.concatenate([second, 0 * third])])

    reach = np.zeros((block, 16))
    reach[:, :TERMS] = polys((token + 1).astype(np.float64)).T
    first, second, _ = parts(reach)
    none = 0 * first
    cross = np.concatenate([first, second] + [none] * 6, axis=1)
    return toeplitz, moments, cross


def one_minus_exp_neg(u):
    series = 1.0 - u * (1.0 / 8.0)
    for n in (7, 6, 5, 4, 3, 2):
        series = 1.0 - (u * (1.0 / n)) * series
    return jnp.where(u < 0.25, u * series, 1.0 - jnp.exp(-u))


def kernel(
    nz,
    ns,
    taps_hbm,
    decay_hbm,
    res_hbm,
    skip_hbm,
    toep_hbm,
    mom_hbm,
    cross_hbm,
    feat_ref,
    out_ref,
    taps_ref,
    decay_ref,
    res_ref,
    skip_ref,
    toep_ref,
    mom_ref,
    cross_ref,
    feats,
    halo_wide,
    halo_send,
    halo_recv,
    halo_past,
    edge_out,
    edges,
    z_out,
    g_out,
    h_src,
    h_col,
    h_all,
    c_keep,
    wide,
    z_keep,
    g_keep,
    u_keep,
    y_keep,
    e_stage,
    e_recv,
    p_keep,
    t_stage,
    t_recv,
    r_stage,
    r_recv,
    r_flat,
    o_wide,
    o_keep,
    arg_sem,
    local_sem,
    z_ssem,
    z_rsem,
    g_ssem,
    g_rsem,
    edge_ssem,
    edge_rsem,
    halo_ssem,
    halo_rsem,
    a_ssem,
    a_rsem,
    b_ssem,
    b_rsem,
    e_ssem,
    e_rsem,
    t_ssem,
    t_rsem,
    r_ssem,
    r_rsem,
    o_lsem,
    o_ssem,
    o_rsem,
):
    modes = decay_hbm.shape[0]
    share = 16 // ns
    rows = feat_ref.shape[1]
    block = 2 * rows
    steps = rows // RUNS
    pairs = nz // 2
    chan = lax.axis_index("chan")
    seq = lax.axis_index("seq")
    z = chan // 2
    k = chan % 2
    other = 1 - k
    position = seq * nz + z
    first = position == 0
    last = position == nz * ns - 1
    f32 = jnp.float32

    def dev(zz, kk, ss):
        return {"chan": zz * 2 + kk, "seq": ss}

    def remote(src, dst, ssem, rsem, device):
        return pltpu.make_async_remote_copy(
            src_ref=src, dst_ref=dst, send_sem=ssem, recv_sem=rsem, device_id=device, device_id_type=MESH
        )

    def local(src, dst, sem):
        return pltpu.make_async_copy(src, dst, sem)

    def wait_bytes(ref, sem):
        pltpu.make_async_copy(ref, ref, sem).wait()

    def far_first(n, of=nz):
        return (of // 2 + ((n + 1) // 2) * (1 - 2 * (n % 2))) % of

    def cols(j, kk):
        return pl.ds(pl.multiple_of((2 * j + kk) * LANES, LANES), LANES)

    my_rows = pl.ds(pl.multiple_of(k * rows, rows), rows)
    other_rows = pl.ds(pl.multiple_of(other * rows, rows), rows)

    barrier = pltpu.get_barrier_semaphore()

    def hello(device):
        pl.semaphore_signal(barrier, inc=1, device_id=device, device_id_type=MESH)

    for n in range(nz - 1):
        hello(dev((z + far_first(n)) % nz, k, seq))
    for n in range(1, ns):
        hello(dev(z, k, (seq + n) % ns))
    hello(dev(z, other, seq))
    before = position - 1 + nz * ns
    after = position + 1

    @pl.when(jnp.logical_not(first))
    def _():
        hello(dev(before % nz, 1, (before // nz) % ns))

    sends_halo = jnp.logical_and(k == 1, jnp.logical_not(last))

    wide_cols = 4 * LANES

    def chunk(p):
        at = pl.ds(pl.multiple_of(p * wide_cols, wide_cols), wide_cols)
        return local(feat_ref.at[:, :, at], feats.at[p], local_sem.at[p])

    def fetch(p, c):
        chunk(p).start()
        return c

    left, right = slice(0, block), slice(block, 2 * block)
    smalls = [
        (taps_hbm, taps_ref.at[pl.ds(0, 3)]),
        (decay_hbm, decay_ref),
        (res_hbm, res_ref),
        (skip_hbm, skip_ref),
        (mom_hbm.at[0], mom_ref.at[:, left]),
        (mom_hbm.at[1], mom_ref.at[:, right]),
        (toep_hbm.at[0], toep_ref.at[:, left]),
        (toep_hbm.at[1], toep_ref.at[:, right]),
        (cross_hbm, cross_ref),
    ]

    def ready(numbers):
        for i in numbers:
            local(*smalls[i], arg_sem.at[i]).wait()

    local(*smalls[0], arg_sem.at[0]).start()
    lax.fori_loop(0, pairs, fetch, 0)
    for i, (src, dst) in enumerate(smalls[1:]):
        local(src, dst, arg_sem.at[1 + i]).start()
    ready((0,))

    row_id = lax.broadcasted_iota(jnp.int32, (RUNS, LANES), 0)

    def spread(row):
        return jnp.broadcast_to(row, (RUNS, LANES))

    def run_rows(i, base=0):
        return pl.ds(base + i, RUNS, stride=steps)

    def conv(p, c):
        chunk(p).wait()
        for h in range(2):
            j = 2 * p + h
            for mine in (True, False):
                kk = k if mine else other
                at = pl.ds(pl.multiple_of((2 * h + kk) * LANES, LANES), LANES)
                streams = []
                for q in range(3):
                    wide[q] = feats[p, q, :, at].astype(f32)
                    tap = [spread(taps_ref[q, t : t + 1, cols(j, kk)]) for t in range(3)]
                    own = [wide[q, run_rows(i), :] for i in range(steps)]
                    seen = [pltpu.roll(own[-2], 1, axis=0), pltpu.roll(own[-1], 1, axis=0)] + own
                    streams.append(
                        [tap[0] * seen[i + 2] + tap[1] * seen[i + 1] + tap[2] * seen[i] for i in range(steps)]
                    )
                    ends = [wide[q, 0:2, :], wide[q, rows - 2 : rows, :]]
                    kept = edges.at[k] if mine else edge_out
                    kept[j, q, 0:2, :] = ends[0]
                    kept[j, q, 2:4, :] = ends[1]
                    halo_wide[kk, pl.ds(j * 6 + 2 * q, 2), :] = ends[1]
                gate = jnp.concatenate(streams[0], axis=0).astype(jnp.bfloat16)
                product = jnp.concatenate([streams[1][i] * streams[2][i] for i in range(steps)], axis=0)
                product = product.astype(jnp.bfloat16)
                lanes = pl.ds(h * LANES, LANES)
                if mine:
                    z_keep[p, my_rows, lanes] = product
                    g_keep[j, my_rows, :] = gate
                else:
                    z_out[p, :, lanes] = product
                    g_out[j] = gate
        return c

    lax.fori_loop(0, pairs, conv, 0)
    halo_send[...] = halo_wide[:, 0 : 6 * nz, :].astype(jnp.bfloat16)

    ready((1, 2, 3))
    decay = decay_ref[...]
    weight = res_ref[...] * jnp.sqrt(one_minus_exp_neg(2.0 * decay))
    half_a = decay * (block / 4.0)
    square = half_a * half_a
    lead = jnp.exp(-2.0 * half_a)
    for t in range(TERMS):
        total = jnp.ones_like(square)
        for i in range(10, 0, -1):
            total = 1.0 + square * (1.0 / (i * (i + t))) * total
        coef = lead * total * (1.0 if t == 0 else 2.0)
        lead = lead * half_a * (-1.0 / (t + 1))
        c_keep[0, t] = coef
        c_keep[1, t] = weight * coef
        h_src[t] = jnp.sum(weight * coef, axis=0, keepdims=True)
    for t in range(TERMS, 16):
        h_src[t] = skip_ref[...]
    r_flat[...] = jnp.zeros_like(r_flat)

    pl.semaphore_wait(barrier, (nz - 1) + (ns - 1) + 1 + 2 * sends_halo.astype(jnp.int32))

    @pl.when(sends_halo)
    def _():
        for kk in range(2):
            remote(
                halo_send.at[kk], halo_recv, halo_ssem, halo_rsem, dev(after % nz, kk, (after // nz) % ns)
            ).start()

    edge_copy = remote(edge_out.at[pl.ds(0, nz)], edges.at[k], edge_ssem, edge_rsem, dev(z, other, seq))
    edge_copy.start()

    def z_copy(p):
        return remote(z_out.at[p], z_keep.at[p, my_rows, :], z_ssem, z_rsem.at[p], dev(z, other, seq))

    def swap(n, c):
        z_copy((z // 2 + far_first(n, pairs)) % pairs).start()
        return c

    lax.fori_loop(0, pairs, swap, 0)

    my_rows_h = h_src.at[pl.ds(seq * share, share)]

    def send_a(n, c):
        remote(my_rows_h, h_col.at[z], a_ssem, a_rsem, dev((z + far_first(n)) % nz, k, seq)).start()
        return c

    lax.fori_loop(0, nz - 1, send_a, 0)
    local(my_rows_h, h_col.at[z], a_rsem).start()

    remote(g_out, g_keep.at[:, my_rows, :], g_ssem, g_rsem, dev(z, other, seq)).start()

    @pl.when(first)
    def _():
        halo_past[...] = jnp.zeros_like(halo_past)

    @pl.when(jnp.logical_not(first))
    def _():
        wait_bytes(halo_recv, halo_rsem)
        halo_past[0 : 6 * nz, :] = halo_recv[...].astype(f32)

    ready((4, 5))
    wait_bytes(edge_out.at[pl.ds(0, nz)], edge_rsem)

    def two_first(q, j, h):
        now = edges[h, j, q, 0:2, :]
        past = halo_past[pl.ds(j * 6 + 2 * q, 2), :] if h == 0 else edges[0, j, q, 2:4, :]
        tap = [taps_ref[q, t : t + 1, cols(j, k)] for t in range(3)]
        one = tap[0] * now[0:1] + tap[1] * past[1:2] + tap[2] * past[0:1]
        two = tap[0] * now[1:2] + tap[1] * now[0:1] + tap[2] * past[1:2]
        return one, two

    tile_row = lax.broadcasted_iota(jnp.int32, (16, LANES), 0)

    def mend(old, one, two):
        fresh = jnp.where(tile_row == 0, jnp.broadcast_to(one, (16, LANES)), old.astype(f32))
        fresh = jnp.where(tile_row == RUNS, jnp.broadcast_to(two, (16, LANES)), fresh)
        return fresh.astype(jnp.bfloat16)

    def forward(n, c):
        p = (z // 2 + far_first(n, pairs)) % pairs
        wait_bytes(z_out.at[p], z_rsem.at[p])
        for h in range(2):
            lanes = pl.ds(h * LANES, LANES)
            for core in range(2):
                at = pl.ds(core * rows, 16)
                second, third = two_first(1, 2 * p + h, core), two_first(2, 2 * p + h, core)
                z_keep[p, at, lanes] = mend(z_keep[p, at, lanes], second[0] * third[0], second[1] * third[1])
        kept = z_keep[p]
        found = jnp.dot(mom_ref[...], jnp.concatenate([kept, kept], axis=0), preferred_element_type=f32)
        found = found[0:16] + found[16:32]
        for h in range(2):
            j = 2 * p + h
            e_stage[j] = found[:, h * LANES : (h + 1) * LANES].astype(jnp.bfloat16)

            @pl.when(j != z)
            def _():
                remote(e_stage.at[j], e_recv.at[z], e_ssem, e_rsem, dev(j, k, seq)).start()

            @pl.when(j == z)
            def _():
                local(e_stage.at[j], e_recv.at[z], e_rsem).start()

        return c

    lax.fori_loop(0, pairs, forward, 0)

    def inner(p, c):
        kept = z_keep[p]
        u_keep[...] = jnp.dot(
            toep_ref[...], jnp.concatenate([kept, kept], axis=0), preferred_element_type=f32
        )
        for h in range(2):
            j = 2 * p + h
            for core in range(2):
                at = pl.ds(core * rows, 16)
                one, two = two_first(0, j, core)
                g_keep[j, at, :] = mend(g_keep[j, at, :], one, two)
            lanes = slice(h * LANES, (h + 1) * LANES)
            hs = [spread(h_all[t // share, j, t % share]) for t in range(TERMS)]
            skip = spread(h_all[TERMS // share, j, TERMS % share])
            for i in range(0, 2 * steps, 2):
                kept = z_keep[p, i * RUNS : (i + 2) * RUNS, lanes].astype(f32)
                for b in range(2):
                    row = (i + b) * RUNS
                    total = skip * kept[b * RUNS : (b + 1) * RUNS]
                    for t in range(TERMS):
                        total = total + hs[t] * u_keep[t * block + row : t * block + row + RUNS, lanes]
                    y_keep[j, row : row + RUNS, :] = total
        return c

    wait_bytes(h_col, a_rsem)

    def send_b(n, c):
        remote(h_col, h_all.at[seq], b_ssem, b_rsem, dev(z, k, (seq + n) % ns)).start()
        return c

    lax.fori_loop(1, ns, send_b, 0)
    local(h_col, h_all.at[seq], b_rsem).start()

    wait_bytes(e_recv, e_rsem)
    block_decay = jnp.exp(-decay * float(block))

    def along_z(zz, state):
        p_keep[zz] = state
        got = e_recv[zz].astype(f32)
        added = c_keep[0, 0] * got[0:1]
        for t in range(1, TERMS):
            added = added + c_keep[0, t] * got[t : t + 1]
        return block_decay * state + added

    t_stage[...] = lax.fori_loop(0, nz, along_z, jnp.zeros_like(decay)).astype(jnp.bfloat16)

    def send_t(ss, c):
        remote(t_stage, t_recv.at[seq], t_ssem.at[ss], t_rsem.at[seq], dev(z, k, ss)).start()
        return c

    lax.fori_loop(seq + 1, ns, send_t, 0)

    seq_decay = jnp.exp(-decay * float(block * nz))

    def along_s(ss, state):
        wait_bytes(t_recv.at[ss], t_rsem.at[ss])
        return seq_decay * state + t_recv[ss].astype(f32)

    incoming = lax.fori_loop(0, seq, along_s, jnp.zeros_like(decay))

    def send_r(n, c):
        zz = (z + far_first(n)) % nz
        state = p_keep[zz] + jnp.exp(-decay * (zz * block).astype(f32)) * incoming
        for t in range(TERMS):
            r_flat[t : t + 1, :] = jnp.sum(c_keep[1, t] * state, axis=0, keepdims=True)
        r_stage[zz] = r_flat[...].astype(jnp.bfloat16)

        @pl.when(n < nz - 1)
        def _():
            remote(r_stage.at[zz], r_recv.at[z], r_ssem, r_rsem.at[z], dev(zz, k, seq)).start()

        @pl.when(n == nz - 1)
        def _():
            local(r_stage.at[zz], r_recv.at[z], r_rsem.at[z]).start()

        return c

    lax.fori_loop(0, nz, send_r, 0)
    wait_bytes(h_all, b_rsem)
    wait_bytes(g_out, g_rsem)
    ready((6, 7, 8))
    lax.fori_loop(0, pairs, inner, 0)

    def finish(n, c):
        p = (z // 2 + far_first(pairs - 1 - n, pairs)) % (pairs)
        for h in range(2):
            j = 2 * p + h
            wait_bytes(r_recv.at[j], r_rsem.at[j])
        coef = jnp.concatenate([r_recv[2 * p], r_recv[2 * p + 1]], axis=1)
        none = jnp.zeros_like(coef)
        stacked = jnp.concatenate([coef, coef] + [none] * 6, axis=0)
        reached = jnp.dot(cross_ref[...], stacked, preferred_element_type=f32)
        for h in range(2):
            j = 2 * p + h
            for i in range(0, 2 * steps, 2):
                gate = g_keep[j, i * RUNS : (i + 2) * RUNS, :].astype(f32)
                for b in range(2):
                    at = slice((i + b) * RUNS, (i + b + 1) * RUNS)
                    half, step = (i + b) // steps, (i + b) % steps
                    o_wide[h, run_rows(step, half * rows), :] = gate[b * RUNS : (b + 1) * RUNS] * (
                        y_keep[j, at, :] + reached[at, h * LANES : (h + 1) * LANES]
                    )
            o_keep[j] = o_wide[h].astype(jnp.bfloat16)
            local(o_keep.at[j, my_rows, :], out_ref.at[:, cols(j, k)], o_lsem).start()
            remote(
                o_keep.at[j, other_rows, :], out_ref.at[:, cols(j, k)], o_ssem, o_rsem, dev(z, other, seq)
            ).start()
        return c

    lax.fori_loop(0, pairs, finish, 0)

    half = out_ref.at[:, pl.ds(0, nz * LANES)]
    wait_bytes(half, o_lsem)
    wait_bytes(half, o_ssem)
    wait_bytes(half, o_rsem)
    wait_bytes(z_out, z_ssem)
    wait_bytes(g_out, g_ssem)
    wait_bytes(edge_out.at[pl.ds(0, nz)], edge_ssem)
    wait_bytes(h_col.at[pl.ds(0, nz - 1)], a_ssem)
    wait_bytes(h_all.at[pl.ds(0, ns - 1)], b_ssem)
    wait_bytes(e_recv.at[pl.ds(0, nz - 1)], e_ssem)

    def sent_t(ss, c):
        wait_bytes(t_stage, t_ssem.at[ss])
        return c

    lax.fori_loop(seq + 1, ns, sent_t, 0)
    wait_bytes(r_recv.at[pl.ds(0, nz - 1)], r_ssem)

    @pl.when(sends_halo)
    def _():
        wait_bytes(halo_send, halo_ssem)


def per_device(nz, ns, features, short_taps, decay_rates, residues, skip_gain):
    streams, rows, width = features.shape
    modes = decay_rates.shape[0]
    block = 2 * rows
    pairs = nz // 2
    toeplitz, moments, cross = fixed_matrices(block)
    f32 = jnp.float32
    bf16 = jnp.bfloat16
    hbm = pl.BlockSpec(memory_space=pltpu.HBM)
    anywhere = pl.BlockSpec(memory_space=pl.ANY)
    dma = pltpu.SemaphoreType.DMA
    return pl.pallas_call(
        functools.partial(kernel, nz, ns),
        out_shape=jax.ShapeDtypeStruct((rows, width), jnp.bfloat16),
        in_specs=[hbm] * 8,
        out_specs=anywhere,
        scratch_shapes=[
            pltpu.VMEM((4,) + short_taps.shape[1:], f32),
            pltpu.VMEM((modes, LANES), f32),
            pltpu.VMEM((modes, LANES), f32),
            pltpu.VMEM((1, LANES), f32),
            pltpu.VMEM((TERMS * block, 2 * block), bf16),
            pltpu.VMEM((32, 2 * block), bf16),
            pltpu.VMEM(cross.shape, bf16),
            pltpu.VMEM((pairs, streams, rows, 4 * LANES), bf16),
            pltpu.VMEM((2, nz * 2 * streams + 16, LANES), f32),
            pltpu.VMEM((2, nz * 2 * streams, LANES), bf16),
            pltpu.VMEM((nz * 2 * streams, LANES), bf16),
            pltpu.VMEM((nz * 2 * streams + 16, LANES), f32),
            pltpu.VMEM((nz + 1, streams, 4, LANES), f32),
            pltpu.VMEM((3, nz, streams, 4, LANES), f32),
            pltpu.VMEM((pairs, rows, 2 * LANES), bf16),
            pltpu.VMEM((nz, rows, LANES), bf16),
            pltpu.VMEM((24, 1, LANES), f32),
            pltpu.VMEM((nz, 16 // ns, 1, LANES), f32),
            pltpu.VMEM((ns, nz, 16 // ns, 1, LANES), f32),
            pltpu.VMEM((2, TERMS, modes, LANES), f32),
            pltpu.VMEM((streams + 1, rows, LANES), f32),
            pltpu.VMEM((pairs, block, 2 * LANES), bf16),
            pltpu.VMEM((nz, block, LANES), bf16),
            pltpu.VMEM((TERMS * block, 2 * LANES), f32),
            pltpu.VMEM((nz, block, LANES), f32),
            pltpu.VMEM((nz, 16, LANES), bf16),
            pltpu.VMEM((nz, 16, LANES), bf16),
            pltpu.VMEM((nz, modes, LANES), f32),
            pltpu.VMEM((modes, LANES), bf16),
            pltpu.VMEM((ns, modes, LANES), bf16),
            pltpu.VMEM((nz, 16, LANES), bf16),
            pltpu.VMEM((nz, 16, LANES), bf16),
            pltpu.VMEM((16, LANES), f32),
            pltpu.VMEM((3, block, LANES), f32),
            pltpu.VMEM((nz, block, LANES), bf16),
            dma((9,)),
            dma((pairs,)),
            dma,
            dma((pairs,)),
            dma,
            dma,
            dma,
            dma,
            dma,
            dma,
            dma,
            dma,
            dma,
            dma,
            dma,
            dma,
            dma((ns,)),
            dma((ns,)),
            dma,
            dma((nz,)),
            dma,
            dma,
            dma,
        ],
        compiler_params=pltpu.CompilerParams(
            collective_id=0, has_side_effects=True, vmem_limit_bytes=60 * 1024 * 1024
        ),
        cost_estimate=pl.CostEstimate(flops=40_000_000, bytes_accessed=2_200_000, transcendentals=0),
    )(short_taps, decay_rates, residues, skip_gain.reshape(1, -1), toeplitz, moments, cross, features)


def solution(mesh):
    nz, ns = mesh.shape["chan"] // 2, mesh.shape["seq"]
    placed = (P(None, ("seq", "chan"), None), P(), P(None, "chan"), P(None, "chan"), P("chan"))
    return jax.shard_map(
        functools.partial(per_device, nz, ns),
        mesh=mesh,
        in_specs=placed,
        out_specs=P(("seq", "chan"), None),
        check_vma=False,
    )
```
